32 devices in a mesh: dp: 32 (over z, y, x, core).
Axes of the slice: x: 2, y: 2, z: 4, core: 2. Of those that a mesh axis runs over, the one named last changes fastest.
Arguments:
- layer_input: bfloat16 [4096, 1024], P('dp'), may hold values from -6 to 6
- qkv_weight: bfloat16 [1024, 3072], P('dp'), may hold values from -0.25 to 0.25
- proj_weight: bfloat16 [1024, 1024], P(None, 'dp'), may hold values from -0.5 to 0.5
- wide_weight: bfloat16 [1024, 5248], P('dp'), may hold values from -0.1875 to 0.1875
- narrow_weight: bfloat16 [2624, 1024], P(None, 'dp'), may hold values from -0.25 to 0.25
- first_gain: bfloat16 [1024], P('dp'), may hold values from 0.099609375 to 1.8984375
- second_gain: bfloat16 [1024], P('dp'), may hold values from 0.099609375 to 1.8984375
- output_grad: float32 [4096, 1024], P('dp'), may hold values from -6 to 6
- document_starts: int32 [1, 21], replicated, may hold values from 0 to 4096, as said below
Outputs:
- layer_output: bfloat16 [4096, 1024], P('dp')
- input_grad: float32 [4096, 1024], P('dp')
- qkv_grad: float32 [1024, 3072], P('dp')
- proj_grad: float32 [1024, 1024], P(None, 'dp')
- wide_grad: float32 [1024, 5248], P('dp')
- narrow_grad: float32 [2624, 1024], P(None, 'dp')
- first_gain_grad: float32 [1024], P('dp')
- second_gain_grad: float32 [1024], P('dp')
The draws below stay inside these ranges and needn't reach their ends.
Inputs may be any that keep to these rules, and one draw needn't show every extreme that they name: `document_starts`: row s lists the first places, within sequence s of 4096 tokens, of its 21 document slots: the first entry is 0, and consecutive entries differ by 200 to 2000 until they reach 4096, where they stay; slots that start at 4096 hold no token, and the last document is cut at the sequence's end.
All inputs are finite; a program needn't handle non-finite values.
Results may differ from the reference program's by a relative error of at most 0.015.
The reference program's roundings to bfloat16 on the way count: a program that leaves them out, or rounds other values in their place, can miss the bound.
Values may be sent and summed in bfloat16 or wider, within the bound.
No kernel may reach another device: no remote copies, remote signals or barrier semaphores. Data moves between devices by JAX's collectives and lax.ppermute only.
A program may use at most 256 MiB of HBM per device.

```python
import jax
import jax.numpy as jnp
from jax import lax

D = 1024
HEADS = 16
HEAD_DIM = 64
FF = 2624
HALF = 64
MIN_DOC = 200
MAX_DOC = 2000
NSEQ = 1
TOKENS = 4096
SEQ = 4096
NDOC = 21


def draw_document_starts(key, part):
    key = jax.random.fold_in(key, 7)
    doc_lengths = jax.random.randint(key, (NSEQ, NDOC - 1), MIN_DOC, MAX_DOC + 1).astype(jnp.int32)
    running = jnp.cumsum(doc_lengths, axis=1).astype(jnp.int32)
    running = jnp.minimum(running, SEQ).astype(jnp.int32)
    leading = jnp.zeros((NSEQ, 1), jnp.int32)
    return jnp.concatenate([leading, running], axis=1)


def spiked(values, key, source, target, parts, factor):
    owner, partner = [(jnp.arange(values.shape[dim]) // (values.shape[dim] // parts)).reshape([-1 if axis == dim else 1 for axis in range(values.ndim)]) for dim in (source, target)]
    chosen = jax.random.permutation(key, parts)[partner]
    strong = (owner == chosen) | (owner == (partner + parts // 2) % parts)
    return jnp.where(strong, factor * values, values)


def level_of(stream_key, dims, pieces, smallest, high):
    gain, own = 1.0, jax.random.fold_in(stream_key, 6)
    for position, parts in pieces:
        heights = jnp.exp(jax.random.uniform(jax.random.fold_in(own, position), (parts,), jnp.float32, smallest / len(pieces), high / len(pieces)))
        gain = gain * jnp.repeat(heights, dims[position] // parts).reshape([-1 if axis == position else 1 for axis in range(len(dims))])
    return gain


def centred(rng, extent, width, most, cuts=(), kind=jnp.bfloat16):
    loudness = level_of(rng, extent, cuts, -0.22, 0.18) if cuts else 1.0
    values = jax.random.normal(rng, extent, jnp.float32) * width * loudness
    return jnp.minimum(jnp.maximum(values, -most), most).astype(kind)


def gaussian_with(key, dims, scale, limit, shards, heavy, kind=jnp.bfloat16):
    values = scale * jax.random.normal(key, dims, jnp.float32)
    if shards:
        values = values * level_of(key, dims, shards, -0.22, 0.18)
    return jnp.clip(spiked(values, jax.random.fold_in(key, 3), *heavy), -limit, limit).astype(kind)


def setup_inputs(seed: int = 0) -> dict:
    splits = jax.random.split(jax.random.key(seed), 10)
    return {
        "layer_input": centred(splits[0], (TOKENS, D), 1.0, 6.0, ((0, 32),)),
        "qkv_weight": centred(splits[1], (D, 3 * D), (D // 2) ** -0.5, 0.25, ((0, 32),)),
        "proj_weight": centred(splits[2], (D, D), (D // 8) ** -0.5, 0.5, ((1, 32),)),
        "wide_weight": centred(splits[3], (D, 2 * FF), D ** -0.5, 0.1875, ((0, 32),)),
        "narrow_weight": centred(splits[4], (FF, D), (FF // 4) ** -0.5, 0.25, ((1, 32),)),
        "first_gain": jnp.clip(1.0 + 0.18 * jax.random.normal(splits[5], (D,), jnp.float32), 0.099609375, 1.8984375).astype(jnp.bfloat16),
        "second_gain": jnp.clip(1.0 + 0.18 * jax.random.normal(splits[6], (D,), jnp.float32), 0.099609375, 1.8984375).astype(jnp.bfloat16),
        "output_grad": gaussian_with(splits[7], (TOKENS, D), 1.0, 6.0, ((0, 32),), (0, 1, 32, 2.75), jnp.float32),
        "document_starts": draw_document_starts(jax.random.fold_in(splits[9], 71), 0),
    }


norm_eps = 1e-05
rope_base = 10000.0

@jax.custom_vjp
def low(v):
    return lax.optimization_barrier(v.astype(jnp.bfloat16)).astype(jnp.float32)

@jax.custom_vjp
def low_back(v):
    return v

def low_keep(v):
    return (low(v), None)

def low_pass(kept, grad):
    return (grad,)

def back_keep(v):
    return (v, None)

def back_low(kept, grad):
    return (low(grad),)
low.defvjp(low_keep, low_pass)
low_back.defvjp(back_keep, back_low)

def layer_norm(values, norm_gain):
    centre = values - lax.optimization_barrier(jnp.mean(values, axis=-1, keepdims=True))
    spread = lax.optimization_barrier(jnp.mean(centre * centre, axis=-1, keepdims=True))
    return centre * lax.rsqrt(spread + norm_eps) * norm_gain

def rope_tables(doc_place):
    freq = rope_base ** (-(2.0 * jnp.arange(HEAD_DIM // 2, dtype=jnp.float32)) / HEAD_DIM)
    angles = doc_place.astype(jnp.float32)[:, None] * freq[None, :]
    angles = jnp.concatenate([angles, angles], axis=1)
    return (jnp.cos(angles), jnp.sin(angles))

def rotate(values, cosine_table, sine_table):
    half_size = values.shape[-1] // 2
    turned = jnp.concatenate([-values[..., half_size:], values[..., :half_size]], axis=-1)
    return values * cosine_table[:, None, :] + turned * sine_table[:, None, :]

def reference(layer_input, qkv_weight, proj_weight, wide_weight, narrow_weight, first_gain, second_gain, output_grad, document_starts):
    highest = lax.Precision.HIGHEST
    score_scale = HEAD_DIM ** (-0.5)
    block_rows = 512
    token_ids = jnp.arange(TOKENS, dtype=jnp.int32)
    sequence = token_ids // SEQ
    places = token_ids % SEQ
    starts = jnp.take(document_starts, sequence, axis=0)
    passed = starts <= places[:, None]
    segment = sequence * (NDOC + 1) + lax.optimization_barrier(jnp.sum(passed.astype(jnp.int32), axis=1))
    doc_place = places - lax.optimization_barrier(jnp.max(jnp.where(passed, starts, 0), axis=1))
    cosine_table, sine_table = rope_tables(doc_place)
    segment_pad = jnp.pad(segment, (HALF, HALF), constant_values=-1)
    query_ids = jnp.arange(block_rows, dtype=jnp.int32)
    key_ids = jnp.arange(block_rows + 2 * HALF, dtype=jnp.int32)
    window = jnp.abs(query_ids[:, None] + HALF - key_ids[None, :]) <= HALF

    def forward(inputs, qkv_matrix, proj_matrix, wide_matrix, narrow_matrix, gain_one, gain_two):
        normed_one = low(layer_norm(inputs, gain_one))
        projected = low_back(jnp.dot(normed_one, qkv_matrix, precision=highest))
        queries = projected[:, :D].reshape(TOKENS, HEADS, HEAD_DIM)
        keys_all = projected[:, D:2 * D].reshape(TOKENS, HEADS, HEAD_DIM)
        values_all = projected[:, 2 * D:].reshape(TOKENS, HEADS, HEAD_DIM)
        query_low = low(rotate(queries, cosine_table, sine_table))
        key_low = low(rotate(keys_all, cosine_table, sine_table))
        value_low = low(values_all)
        key_pad = jnp.pad(key_low, ((HALF, HALF), (0, 0), (0, 0)))
        value_pad = jnp.pad(value_low, ((HALF, HALF), (0, 0), (0, 0)))

        def attend(index):
            start = (index * block_rows).astype(jnp.int32)
            query_block = lax.dynamic_slice_in_dim(query_low, start, block_rows, 0)
            key_block = lax.dynamic_slice_in_dim(key_pad, start, block_rows + 2 * HALF, 0)
            value_block = lax.dynamic_slice_in_dim(value_pad, start, block_rows + 2 * HALF, 0)
            query_seg = lax.dynamic_slice_in_dim(segment, start, block_rows, 0)
            key_seg = lax.dynamic_slice_in_dim(segment_pad, start, block_rows + 2 * HALF, 0)
            allowed = window & (query_seg[:, None] == key_seg[None, :])
            scores = jnp.einsum('qhd,khd->hqk', query_block, key_block, precision=highest) * score_scale
            scores = low_back(scores)
            scores = jnp.where(allowed[None], scores, -1e+30)
            row_top = lax.optimization_barrier(jnp.max(scores, axis=-1, keepdims=True))
            raised = jnp.where(allowed[None], jnp.exp(scores - row_top), 0.0)
            probs = low(raised / lax.optimization_barrier(jnp.sum(raised, axis=-1, keepdims=True)))
            attended = jnp.einsum('hqk,khd->qhd', probs, value_block, precision=highest).reshape(block_rows, D)
            return low(low_back(attended))
        attended = lax.map(jax.checkpoint(attend), jnp.arange(TOKENS // block_rows, dtype=jnp.int32))
        attended = attended.reshape(TOKENS, D)
        branch_one = low_back(jnp.dot(attended, proj_matrix, precision=highest))
        middle = inputs + branch_one
        normed_two = low(layer_norm(middle, gain_two))
        both = low_back(jnp.dot(normed_two, wide_matrix, precision=highest))
        product = low(jax.nn.gelu(both[:, :FF], approximate=False) * both[:, FF:])
        branch_two = low_back(jnp.dot(product, narrow_matrix, precision=highest))
        return middle + branch_two
    result, pull = jax.vjp(forward, layer_input.astype(jnp.float32), qkv_weight.astype(jnp.float32), proj_weight.astype(jnp.float32), wide_weight.astype(jnp.float32), narrow_weight.astype(jnp.float32), first_gain.astype(jnp.float32), second_gain.astype(jnp.float32))
    grads = pull(output_grad.astype(jnp.float32))
    return (result.astype(jnp.bfloat16), grads[0], grads[1], grads[2], grads[3], grads[4], grads[5], grads[6])
```

```python
import jax
import jax.numpy as jnp
from jax import lax
from jax.experimental import pallas as pl
from jax.experimental.pallas import tpu as pltpu
from jax.sharding import PartitionSpec as P

D = 1024
HEADS = 16
HEAD_DIM = 64
FF = 2624
HALF = 64
LANES = 128

norm_eps = 1e-05
rope_base = 10000.0
score_scale = HEAD_DIM ** (-0.5)

MAIN = FF // 2 // LANES * LANES
REST = FF // 2 - MAIN
UNITS = (256, 256, 384, 384)
HALF_D = D // 2

bf16 = jnp.bfloat16
f32 = jnp.float32


def dot(left, right):
    return lax.dot_general(left, right, (((1,), (0,)), ((), ())), preferred_element_type=f32)


def dot_rt(left, right):
    return lax.dot_general(left, right, (((1,), (1,)), ((), ())), preferred_element_type=f32)


def dot_lt(left, right):
    return lax.dot_general(left, right, (((0,), (0,)), ((), ())), preferred_element_type=f32)


def swap(value, bit):
    size = lax.axis_size("dp")
    return lax.ppermute(value, "dp", [(i, i ^ bit) for i in range(size)])


def shifted(value, step):
    size = lax.axis_size("dp")
    pairs = [(i, i + 2 * step) for i in range(size) if 0 <= i + 2 * step < size]
    return lax.ppermute(value, "dp", pairs)


def bit_orders(bits):
    if bits == 4:
        return ((3, 2, 0, 1), (3, 2, 1, 0), (0, 3, 2, 1), (1, 3, 2, 0))
    plain = tuple(range(bits))
    return tuple(plain[::-1][i:] + plain[::-1][:i] for i in (0, 1, 2, 3))


def gather_rows(value, order, bits):
    rows, columns = value.shape
    value = value.reshape((1,) * bits + (rows, columns))
    for bit in order:
        other = swap(value, 2 << bit)
        value = jnp.concatenate([value, other], axis=bits - 1 - bit)
    return value.reshape(-1, columns)


def scatter_rows(value, order, bits):
    rows, columns = (value.shape[0] >> bits, value.shape[1])
    value = value.reshape((2,) * bits + (rows, columns))
    for place, bit in enumerate(order[::-1]):
        axis = bits - 1 - bit
        keep = lax.slice_in_dim(value, 0, 1, axis=axis)
        give = lax.slice_in_dim(value, 1, 2, axis=axis)
        value = keep.astype(f32) + swap(give, 2 << bit).astype(f32)
        if place < bits - 1:
            value = value.astype(bf16)
    return value.reshape(rows, columns)


def reorder(value, chip, chips):
    rows, width = value.shape
    block = width // chips
    per_tile = LANES // block

    def kernel(chip_ref, in_ref, out_ref):
        here = chip_ref[0]
        lane = lax.broadcasted_iota(jnp.int32, (rows, LANES), 1)
        for tile in range(width // LANES):
            source = jnp.bitwise_xor(here // per_tile, tile)
            part = in_ref[:, pl.ds(pl.multiple_of(source * LANES, LANES), LANES)].astype(f32)
            step, place = block, 1
            while step < LANES:
                up = pltpu.roll(part, step, 1)
                down = pltpu.roll(part, LANES - step, 1)
                turned = jnp.where((lane & step) != 0, up, down)
                part = jnp.where((here // place) % 2 == 1, turned, part)
                step, place = step * 2, place * 2
            out_ref[:, tile * LANES : (tile + 1) * LANES] = part.astype(out_ref.dtype)

    return pl.pallas_call(
        kernel,
        out_shape=jax.ShapeDtypeStruct(value.shape, value.dtype),
        in_specs=[
            pl.BlockSpec(memory_space=pltpu.SMEM),
            pl.BlockSpec(memory_space=pltpu.VMEM),
        ],
        out_specs=pl.BlockSpec(memory_space=pltpu.VMEM),
        name="reorder",
        compiler_params=pltpu.CompilerParams(vmem_limit_bytes=24 * 2**20),
    )(chip.reshape(1), value)


def turn(value):
    lane = lax.broadcasted_iota(jnp.int32, value.shape, 1)
    first = (lane % HEAD_DIM) < HEAD_DIM // 2
    ahead = pltpu.roll(value, LANES - HEAD_DIM // 2, 1)
    behind = pltpu.roll(value, HEAD_DIM // 2, 1)
    return jnp.where(first, -ahead, behind)


def only_head(value, head):
    lane = lax.broadcasted_iota(jnp.int32, value.shape, 1)
    return jnp.where((lane // HEAD_DIM) == head, value, jnp.zeros_like(value))


def attend_kernel(
    q_ref, k_ref, v_ref, cos_ref, sin_ref, seg_col_ref, seg_row_ref,
    q_low_ref, k_low_ref, v_low_ref, probs_ref, out_ref,
):
    count = q_ref.shape[0]
    cosine, sine = cos_ref[...], sin_ref[...]
    query, key = q_ref[...], k_ref[...]
    inner = slice(HALF, HALF + count)
    q_low_ref[...] = (query * cosine[inner] + turn(query) * sine[inner]).astype(bf16)
    k_low_ref[...] = (key * cosine + turn(key) * sine).astype(bf16)
    v_low_ref[...] = v_ref[...].astype(bf16)
    block = 2 * HALF
    rows = lax.broadcasted_iota(jnp.int32, (block, 2 * block), 0)
    columns = lax.broadcasted_iota(jnp.int32, (block, 2 * block), 1)
    window = jnp.abs(rows + HALF - columns) <= HALF
    lane = lax.broadcasted_iota(jnp.int32, (block, LANES), 1)
    for first in range(0, count, block):
        allowed = window & (
            seg_col_ref[first + HALF : first + HALF + block, :]
            == seg_row_ref[:, first : first + 2 * block]
        )
        query_low = q_low_ref[first : first + block, :]
        key_low = k_low_ref[first : first + 2 * block, :]
        value_low = v_low_ref[first : first + 2 * block, :]
        results = []
        for head in range(2):
            scores = dot_rt(only_head(query_low, head), key_low) * score_scale
            scores = jnp.where(allowed, scores, -1e30)
            top = jnp.max(scores, axis=1, keepdims=True)
            raised = jnp.where(allowed, jnp.exp(scores - top), 0.0)
            probs = raised / jnp.sum(raised, axis=1, keepdims=True)
            probs_ref[head, first : first + block, :] = probs
            results.append(dot(probs.astype(bf16), value_low))
        out_ref[first : first + block, :] = jnp.where(
            lane < HEAD_DIM, results[0], results[1]
        ).astype(bf16)


def attend(query, key, value, cosine, sine, seg_col, seg_row):
    count, extended = query.shape[0], key.shape[0]
    pairs = query.shape[1] // LANES
    column = lambda size: pl.BlockSpec((size, LANES), lambda i: (0, i))
    whole = lambda array: pl.BlockSpec(array.shape, lambda i: (0, 0))
    return pl.pallas_call(
        attend_kernel,
        grid=(pairs,),
        out_shape=(
            jax.ShapeDtypeStruct(query.shape, bf16),
            jax.ShapeDtypeStruct(key.shape, bf16),
            jax.ShapeDtypeStruct(value.shape, bf16),
            jax.ShapeDtypeStruct((2 * pairs, count, 4 * HALF), f32),
            jax.ShapeDtypeStruct(query.shape, bf16),
        ),
        in_specs=[column(count), column(extended), column(extended)]
        + [whole(a) for a in (cosine, sine, seg_col, seg_row)],
        out_specs=(
            column(count),
            column(extended),
            column(extended),
            pl.BlockSpec((2, count, 4 * HALF), lambda i: (i, 0, 0)),
            column(count),
        ),
        name="attend",
        compiler_params=pltpu.CompilerParams(vmem_limit_bytes=32 * 2**20),
    )(query, key, value, cosine, sine, seg_col, seg_row)


def attend_back_kernel(
    grad_ref, probs_ref, q_ref, k_ref, v_ref, cos_ref, sin_ref, dq_ref, dk_ref, dv_ref
):
    count = q_ref.shape[0]
    block = 2 * HALF
    lane = lax.broadcasted_iota(jnp.int32, (block, LANES), 1)
    dk_ref[...] = jnp.zeros_like(dk_ref)
    dv_ref[...] = jnp.zeros_like(dv_ref)
    for first in range(0, count, block):
        grad = grad_ref[first : first + block, :]
        query_low = q_ref[first : first + block, :]
        key_low = k_ref[first : first + 2 * block, :]
        value_low = v_ref[first : first + 2 * block, :]
        results = []
        key_sum = jnp.zeros((2 * block, LANES), f32)
        value_sum = jnp.zeros((2 * block, LANES), f32)
        for head in range(2):
            own_grad = only_head(grad, head)
            probs = probs_ref[head, first : first + block, :]
            probs_grad = dot_rt(own_grad, value_low)
            delta = jnp.sum(probs * probs_grad, axis=1, keepdims=True)
            scores_grad = (probs * (probs_grad - delta)).astype(bf16)
            results.append(dot(scores_grad, key_low))
            key_sum += dot_lt(scores_grad, only_head(query_low, head))
            value_sum += dot_lt(probs.astype(bf16), own_grad)
        dk_ref[first : first + 2 * block, :] += key_sum * score_scale
        dv_ref[first : first + 2 * block, :] += value_sum
        query_grad = jnp.where(lane < HEAD_DIM, results[0], results[1]) * score_scale
        place = slice(first + HALF, first + HALF + block)
        dq_ref[first : first + block, :] = (
            query_grad * cos_ref[place, :] - turn(query_grad * sin_ref[place, :])
        ).astype(bf16)


def attend_back(grad, probs, query, key, value, cosine, sine):
    count, extended = query.shape[0], key.shape[0]
    pairs = query.shape[1] // LANES
    column = lambda size: pl.BlockSpec((size, LANES), lambda i: (0, i))
    whole = lambda array: pl.BlockSpec(array.shape, lambda i: (0, 0))
    return pl.pallas_call(
        attend_back_kernel,
        grid=(pairs,),
        out_shape=(
            jax.ShapeDtypeStruct(query.shape, bf16),
            jax.ShapeDtypeStruct(key.shape, f32),
            jax.ShapeDtypeStruct(value.shape, f32),
        ),
        in_specs=[
            column(count),
            pl.BlockSpec((2, count, 4 * HALF), lambda i: (i, 0, 0)),
            column(count),
            column(extended),
            column(extended),
            whole(cosine),
            whole(sine),
        ],
        out_specs=(column(count), column(extended), column(extended)),
        name="attend_back",
        compiler_params=pltpu.CompilerParams(vmem_limit_bytes=32 * 2**20),
    )(grad, probs, query, key, value, cosine, sine)


def join_kernel(dk_ref, dv_ref, before_k, before_v, after_k, after_v, cos_ref, sin_ref, k_out, v_out):
    count = k_out.shape[0]
    inner = slice(HALF, HALF + count)

    def own(ref, before, after):
        first = ref[HALF : 2 * HALF, :] + before[...].astype(f32)
        middle = ref[2 * HALF : count, :]
        last = ref[count : count + HALF, :] + after[...].astype(f32)
        return jnp.concatenate([first, middle, last], axis=0)

    grad = own(dk_ref, before_k, after_k)
    k_out[...] = (grad * cos_ref[inner, :] - turn(grad * sin_ref[inner, :])).astype(bf16)
    v_out[...] = own(dv_ref, before_v, after_v).astype(bf16)


def join(dk, dv, before, after, cosine, sine):
    extended, width = dk.shape
    count = extended - 2 * HALF
    pairs = width // LANES
    column = lambda size: pl.BlockSpec((size, LANES), lambda i: (0, i))
    second = pl.BlockSpec((HALF, LANES), lambda i: (0, i + pairs))
    whole = lambda array: pl.BlockSpec(array.shape, lambda i: (0, 0))
    return pl.pallas_call(
        join_kernel,
        grid=(pairs,),
        out_shape=(jax.ShapeDtypeStruct((count, width), bf16),) * 2,
        in_specs=[
            column(extended), column(extended), column(HALF), second, column(HALF), second,
            whole(cosine), whole(sine),
        ],
        out_specs=(column(count), column(count)),
        name="join_halo",
        compiler_params=pltpu.CompilerParams(vmem_limit_bytes=32 * 2**20),
    )(dk, dv, before, before, after, after, cosine, sine)


def token_layout(first_token, count, total_tokens, document_starts):
    seq_length = total_tokens // document_starts.shape[0]
    global_ids = first_token + jnp.arange(count, dtype=jnp.int32)
    in_range = (global_ids >= 0) & (global_ids < total_tokens)
    safe_ids = jnp.clip(global_ids, 0, total_tokens - 1)
    sequence = safe_ids // seq_length
    place = safe_ids % seq_length
    starts = jnp.take(document_starts, sequence, axis=0)
    passed = starts <= place[:, None]
    segment = sequence * (document_starts.shape[1] + 1) + jnp.sum(passed.astype(jnp.int32), axis=1)
    segment = jnp.where(in_range, segment, -1)
    doc_place = place - jnp.max(jnp.where(passed, starts, 0), axis=1)
    return (segment, doc_place)


def rope_tables(doc_place):
    freq = rope_base ** (-(2.0 * jnp.arange(HEAD_DIM // 2, dtype=f32)) / HEAD_DIM)
    angles = doc_place.astype(f32)[:, None] * freq[None, :]
    spread = lambda table: jnp.tile(table, (1, LANES * 2 // HEAD_DIM))
    return (spread(jnp.cos(angles)), spread(jnp.sin(angles)))


def norm_parts(values):
    centre = values - jnp.mean(values, axis=-1, keepdims=True)
    spread = jnp.mean(centre * centre, axis=-1, keepdims=True)
    root = lax.rsqrt(spread + norm_eps)
    return (centre * root, root)


def norm_back(grad, gain, hat, root):
    scaled = grad * gain
    return root * (
        scaled
        - jnp.mean(scaled, axis=-1, keepdims=True)
        - hat * jnp.mean(scaled * hat, axis=-1, keepdims=True)
    )


def gated_unit(inner_part, gate_part):
    return jax.nn.gelu(inner_part, approximate=False) * gate_part


def on_device(
    layer_input,
    qkv_weight,
    proj_weight,
    wide_weight,
    narrow_weight,
    first_gain,
    second_gain,
    output_grad,
    document_starts,
):
    size = lax.axis_size("dp")
    chips = size // 2
    bits = chips.bit_length() - 1
    orders = bit_orders(bits)
    device = lax.axis_index("dp").astype(jnp.int32)
    chip, core = device // 2, device % 2
    is_first = core == 0
    rows = layer_input.shape[0]
    tokens = 2 * rows
    own_rows = qkv_weight.shape[0]

    def pick(first, second):
        return (jnp.where(is_first, first, second), jnp.where(is_first, second, first))

    def both_cores(mine, other, axis=0):
        return jnp.where(
            is_first,
            jnp.concatenate([mine, other], axis=axis),
            jnp.concatenate([other, mine], axis=axis),
        )

    def own_half(value):
        return lax.dynamic_slice_in_dim(value, core * (value.shape[0] // 2), value.shape[0] // 2, 0)

    def other_half(value):
        half = value.shape[0] // 2
        return lax.dynamic_slice_in_dim(value, (1 - core) * half, half, 0)

    proj_turned = proj_weight.T
    narrow_turned = narrow_weight.T

    def first_group(which):
        heads = slice(which * HALF_D, (which + 1) * HALF_D)
        part = slice(2 * MAIN + which * REST, 2 * MAIN + (which + 1) * REST)
        return jnp.concatenate(
            [qkv_weight[:, i * D : (i + 1) * D][:, heads] for i in range(3)]
            + [proj_turned[:, heads]]
            + [wide_weight[:, :FF][:, part], wide_weight[:, FF:][:, part], narrow_turned[:, part]]
            + [first_gain[:, None], second_gain[:, None]]
            + [jnp.zeros((own_rows, LANES - 3 * REST - 2), bf16)],
            axis=1,
        )

    def second_group(which):
        parts, at = [], which * MAIN
        for units in UNITS:
            here = slice(at, at + units)
            parts += [wide_weight[:, :FF][:, here], wide_weight[:, FF:][:, here], narrow_turned[:, here]]
            at += units
        return jnp.concatenate(parts, axis=1)

    mine, give = pick(first_group(0), first_group(1))
    group_one = both_cores(mine, swap(give, 1))
    mine, give = pick(second_group(0), second_group(1))
    group_two = both_cores(mine, swap(give, 1))

    pieces_one = (HALF_D, HALF_D, HALF_D, HALF_D + LANES)
    gathered, at = [], 0
    for width, order in zip(pieces_one, orders):
        gathered.append(gather_rows(group_one[:, at : at + width], order, bits))
        at += width
    query_w, key_w, value_w, proj_rest = gathered
    proj_w, rest_w = proj_rest[:, :HALF_D], proj_rest[:, HALF_D:]
    feed, at = [], 0
    for units, order in zip(UNITS, orders):
        feed.append(gather_rows(group_two[:, at : at + 3 * units], order, bits))
        at += 3 * units

    segment, doc_place = token_layout(
        chip * tokens - HALF, tokens + 2 * HALF, rows * size, document_starts
    )
    cosine, sine = rope_tables(doc_place)
    chip_input = both_cores(layer_input, swap(layer_input, 1))
    before = shifted(chip_input[tokens - HALF :], 1)
    after = shifted(chip_input[:HALF], -1)
    inputs = reorder(jnp.concatenate([before, chip_input, after], axis=0), chip, chips)
    out_grad = reorder(both_cores(output_grad, swap(output_grad, 1)), chip, chips)
    out_low = out_grad.astype(bf16)
    inner_rows = slice(HALF, HALF + tokens)

    gain_one = rest_w[:, 3 * REST].astype(f32)
    gain_two = rest_w[:, 3 * REST + 1].astype(f32)
    inputs32 = inputs.astype(f32)
    hat_one, root_one = norm_parts(inputs32)
    normed_ext = (hat_one * gain_one).astype(bf16)
    normed_low = normed_ext[inner_rows]
    query_low, key_low, value_low, probs, attended_low = attend(
        dot(normed_low, query_w),
        dot(normed_ext, key_w),
        dot(normed_ext, value_w),
        cosine,
        sine,
        segment[:, None],
        segment[None, :],
    )
    branch = dot_rt(attended_low, proj_w)
    middle = inputs32[inner_rows] + (branch + swap(branch, 1))

    hat_two, root_two = norm_parts(middle)
    normed_two = (hat_two * gain_two).astype(bf16)
    out_sum = jnp.zeros((tokens, D), f32)
    wide_back = jnp.zeros((tokens, D), f32)
    feed_grads = []

    def unit_part(inner_part, gate_part, product_grad):
        product, pull = jax.vjp(gated_unit, inner_part, gate_part)
        inner_grad, gate_grad = pull(product_grad)
        return (product.astype(bf16), inner_grad.astype(bf16), gate_grad.astype(bf16))

    for units, weight, order in zip(UNITS, feed, orders):
        both = dot(normed_two, weight[:, : 2 * units])
        product, inner_grad, gate_grad = unit_part(
            both[:, :units], both[:, units:], dot(out_low, weight[:, 2 * units :])
        )
        out_sum += dot_rt(product, weight[:, 2 * units :])
        both_grad = jnp.concatenate([inner_grad, gate_grad], axis=1)
        wide_back += dot_rt(both_grad, weight[:, : 2 * units])
        grad = jnp.concatenate(
            [dot_lt(normed_two, both_grad).astype(bf16), dot_lt(out_low, product).astype(bf16)],
            axis=1,
        )
        feed_grads.append(scatter_rows(grad, order, bits))

    rest = dot(normed_two, rest_w[:, : 2 * REST])
    product, inner_grad, gate_grad = unit_part(
        rest[:, :REST], rest[:, REST:], dot(out_low, rest_w[:, 2 * REST : 3 * REST])
    )
    out_sum += dot_rt(product, rest_w[:, 2 * REST : 3 * REST])
    both_grad = jnp.concatenate([inner_grad, gate_grad], axis=1)
    wide_back += dot_rt(both_grad, rest_w[:, : 2 * REST])
    rest_grad = jnp.concatenate(
        [
            dot_lt(normed_two, both_grad).astype(bf16),
            dot_lt(out_low, product).astype(bf16),
            jnp.zeros((D, LANES - 3 * REST), bf16),
        ],
        axis=1,
    )

    wide_back = wide_back + swap(wide_back, 1)
    middle_grad = out_grad + norm_back(wide_back, gain_two, hat_two, root_two)
    middle_low = middle_grad.astype(bf16)
    attended_grad = dot(middle_low, proj_w).astype(bf16)
    proj_grad = dot_lt(middle_low, attended_low).astype(bf16)
    proj_part = scatter_rows(jnp.concatenate([proj_grad, rest_grad], axis=1), orders[3], bits)

    query_grad, key_ext, value_ext = attend_back(
        attended_grad, probs, query_low, key_low, value_low, cosine, sine
    )
    last = tokens + HALF
    rim = lambda part: jnp.concatenate([key_ext[part], value_ext[part]], axis=1).astype(bf16)
    from_before = shifted(rim(slice(last, None)), 1)
    from_after = shifted(rim(slice(0, HALF)), -1)
    key_grad, value_grad = join(key_ext, value_ext, from_before, from_after, cosine, sine)
    qkv_parts = [
        scatter_rows(dot_lt(normed_low, grad).astype(bf16), order, bits)
        for grad, order in zip((query_grad, key_grad, value_grad), orders)
    ]
    first_back = (
        dot_rt(query_grad, query_w) + dot_rt(key_grad, key_w) + dot_rt(value_grad, value_w)
    )
    first_back = own_half(first_back) + swap(other_half(first_back), 1)
    input_grad = own_half(middle_grad) + norm_back(
        first_back, gain_one, own_half(hat_one[inner_rows]), own_half(root_one[inner_rows])
    )
    input_grad = reorder(input_grad, chip, chips)

    out_sum = own_half(out_sum) + swap(other_half(out_sum), 1)
    layer_output = reorder((own_half(middle) + out_sum).astype(bf16), chip, chips)

    def shared(value):
        mine, other = (own_half(value), swap(other_half(value), 1))
        return (jnp.where(is_first, mine, other), jnp.where(is_first, other, mine))

    feed_pair = shared(jnp.concatenate(feed_grads, axis=1))
    proj_pair = shared(proj_part)
    qkv_pair = shared(jnp.concatenate(qkv_parts, axis=1))
    qkv_grad = jnp.concatenate(
        [pair[:, i * HALF_D : (i + 1) * HALF_D] for i in range(3) for pair in qkv_pair], axis=1
    )
    proj_share = jnp.concatenate([pair[:, :HALF_D] for pair in proj_pair], axis=1).T

    def unit_columns(kind):
        columns = []
        for pair in feed_pair:
            at = 0
            for units in UNITS:
                columns.append(pair[:, at + kind * units : at + (kind + 1) * units])
                at += 3 * units
        rest_at = HALF_D + kind * REST
        return columns + [pair[:, rest_at : rest_at + REST] for pair in proj_pair]

    wide_share = jnp.concatenate(unit_columns(0) + unit_columns(1), axis=1)
    narrow_share = jnp.concatenate(unit_columns(2), axis=1).T

    gain_one_share = jnp.sum(qkv_weight.astype(f32) * qkv_grad, axis=1) / first_gain.astype(f32)
    gain_two_share = jnp.sum(wide_weight.astype(f32) * wide_share, axis=1) / second_gain.astype(f32)
    return (
        layer_output,
        input_grad,
        qkv_grad,
        proj_share,
        wide_share,
        narrow_share,
        gain_one_share,
        gain_two_share,
    )


def solution(mesh):
    placed = (
        P("dp", None),
        P("dp", None),
        P(None, "dp"),
        P("dp", None),
        P(None, "dp"),
        P("dp"),
        P("dp"),
        P("dp", None),
        P(),
    )
    return jax.shard_map(
        on_device,
        mesh=mesh,
        in_specs=placed,
        out_specs=(
            P("dp", None),
            P("dp", None),
            P("dp", None),
            P(None, "dp"),
            P("dp", None),
            P(None, "dp"),
            P("dp"),
            P("dp"),
        ),
        check_vma=False,
    )
```

```python
import jax
import jax.numpy as jnp
from jax import lax
from jax.experimental import pallas as pl
from jax.experimental.pallas import tpu as pltpu
from jax.sharding import PartitionSpec as P

D = 1024
HEADS = 16
HEAD_DIM = 64
FF = 2624
HALF = 64
LANES = 128

norm_eps = 1e-05
rope_base = 10000.0
score_scale = HEAD_DIM ** (-0.5)

TEAM = 8
UNITS = FF // TEAM
SPAN = -(-UNITS // LANES) * LANES
BLOCK = 3 * SPAN

bf16 = jnp.bfloat16
f32 = jnp.float32


def dot(left, right):
    return lax.dot_general(left, right, (((1,), (0,)), ((), ())), preferred_element_type=f32)


def dot_rt(left, right):
    return lax.dot_general(left, right, (((1,), (1,)), ((), ())), preferred_element_type=f32)


def dot_lt(left, right):
    return lax.dot_general(left, right, (((0,), (0,)), ((), ())), preferred_element_type=f32)


def swap(value, bit):
    size = lax.axis_size("dp")
    return lax.ppermute(value, "dp", [(i, i ^ bit) for i in range(size)])


def shifted(value, step):
    size = lax.axis_size("dp")
    pairs = [(i, i + TEAM * step) for i in range(size) if 0 <= i + TEAM * step < size]
    return lax.ppermute(value, "dp", pairs)


def after(value, *others):
    return lax.optimization_barrier((value, *others))[0]


def gather_rows(value, order, low, high, gate=None, stages=None):
    rows, columns = value.shape
    value = value.reshape((1,) * (high - low) + (rows, columns))
    for bit in order:
        other = swap(value, 2 << bit)
        if gate is not None and bit == order[0]:
            other = after(other, *gate)
        value = jnp.concatenate([value, other], axis=high - 1 - bit)
        if stages is not None:
            stages.append(value)
    return value.reshape(-1, columns)


def scatter_first(halves, order):
    return swap(halves[1], 2 << order[-1])


def scatter_second(halves, got):
    return (halves[0].astype(f32) + got.astype(f32)).astype(bf16)


def scatter_rows(value, order, low, high, gates=()):
    order = order[::-1]
    left = [bit for bit in range(high - 1, low - 1, -1) if bit != order[0]]
    rows, columns = value.shape[0] >> len(left), value.shape[1]
    value = value.reshape((2,) * len(left) + (rows, columns))
    for bit in order[1:]:
        value = value.astype(bf16)
        axis = left.index(bit)
        keep = lax.slice_in_dim(value, 0, 1, axis=axis)
        give = lax.slice_in_dim(value, 1, 2, axis=axis)
        got = swap(give, 2 << bit)
        if bit == order[-1] and gates:
            got = after(got, *gates)
        value = keep.astype(f32) + got.astype(f32)
    return value.reshape(rows, columns)


def turned_by(value, key, axes):
    for place, axis in enumerate(axes[::-1]):
        value = jnp.where((key >> place) % 2 == 1, jnp.flip(value, axis), value)
    return value


def permuted_tile(ref, rows, tile, key, block):
    per_tile = max(LANES // block, 1)
    if block >= LANES:
        source = jnp.bitwise_xor(key * (block // LANES), tile)
    else:
        source = jnp.bitwise_xor(key // per_tile, tile)
    part = ref[rows, pl.ds(pl.multiple_of(source * LANES, LANES), LANES)].astype(f32)
    lane = lax.broadcasted_iota(jnp.int32, part.shape, 1)
    step, place = block, 1
    while step < LANES:
        up = pltpu.roll(part, step, 1)
        down = pltpu.roll(part, LANES - step, 1)
        part = jnp.where((key // place) % 2 == 1, jnp.where((lane & step) != 0, up, down), part)
        step, place = step * 2, place * 2
    return part


def reorder(value, key, blocks, stacked=False):
    rows, width = value.shape

    def kernel(key_ref, in_ref, out_ref):
        for tile in range(width // LANES):
            part = permuted_tile(in_ref, slice(None), tile, key_ref[0], width // blocks)
            part = part.astype(out_ref.dtype)
            if stacked:
                out_ref[tile * rows : (tile + 1) * rows, :] = part
            else:
                out_ref[:, tile * LANES : (tile + 1) * LANES] = part

    shape = (rows * width // LANES, LANES) if stacked else value.shape
    return pl.pallas_call(
        kernel,
        out_shape=jax.ShapeDtypeStruct(shape, value.dtype),
        in_specs=[
            pl.BlockSpec(memory_space=pltpu.SMEM),
            pl.BlockSpec(memory_space=pltpu.VMEM),
        ],
        out_specs=pl.BlockSpec(memory_space=pltpu.VMEM),
        name="reorder",
        compiler_params=pltpu.CompilerParams(vmem_limit_bytes=8 * 2**20),
    )(key.reshape(1), value)


def kernel_call(kernel, name, shapes, arrays, scratch=(), limit=32, far_out=0):
    space = lambda place: pl.BlockSpec(memory_space=place)
    return pl.pallas_call(
        kernel,
        out_shape=tuple(jax.ShapeDtypeStruct(*shape) for shape in shapes),
        in_specs=[space(pltpu.SMEM)] + [space(pltpu.VMEM)] * (len(arrays) - 1),
        out_specs=(space(pltpu.HBM),) * far_out + (space(pltpu.VMEM),) * (len(shapes) - far_out),
        scratch_shapes=list(scratch),
        name=name,
        compiler_params=pltpu.CompilerParams(vmem_limit_bytes=limit * 2**20),
    )(*arrays)


def token_block(member_ref, place):
    core, chip = member_ref[0] % 2, member_ref[0] // 2
    return ((place % 4) ^ chip) * 2 + ((place // 4) ^ core)


def block_rows(member_ref, place, rows, offset=0):
    at = token_block(member_ref, place) * rows + offset
    return pl.ds(pl.multiple_of(at, min(rows, HALF)), rows)


def pack(scalars, qkv, proj, wide, narrow, gains):
    rows = qkv.shape[0]

    def kernel(scalar_ref, qkv_ref, proj_ref, wide_ref, narrow_ref, gain_ref, mine_ref, give_ref):
        core, chip = scalar_ref[0] % 2, scalar_ref[0] // 2
        lane = lax.broadcasted_iota(jnp.int32, (rows, SPAN), 1)

        def units(ref, start):
            base = start // LANES * LANES
            window = -(-(start - base + UNITS) // LANES) * LANES
            part = ref[:, base : base + window].astype(f32)
            if start > base:
                part = pltpu.roll(part, window - (start - base), 1)
            return jnp.where(lane < UNITS, part[:, :SPAN], 0.0)

        for owner in range(TEAM):
            place = (owner // 2) ^ chip

            def write(ref):
                for i in range(3):
                    at = i * D + owner * LANES
                    ref[place, :, i * LANES : (i + 1) * LANES] = qkv_ref[:, at : at + LANES]
                ref[place, :, 3 * LANES : 4 * LANES] = proj_ref[
                    :, owner * LANES : (owner + 1) * LANES
                ]
                inner = units(wide_ref, owner * UNITS)
                for i in range(2):
                    line = lax.broadcasted_iota(jnp.int32, (rows, SPAN), 0)
                    inner = jnp.where((lane >= UNITS) & (line == i), gain_ref[i : i + 1, :], inner)
                gate = units(wide_ref, FF + owner * UNITS)
                out = units(narrow_ref, owner * UNITS)
                for i, value in enumerate((inner, gate, out)):
                    at = 4 * LANES + i * SPAN
                    ref[place, :, at : at + SPAN] = value.astype(bf16)

            pl.when(core == owner % 2)(lambda: write(mine_ref))
            pl.when(core != owner % 2)(lambda: write(give_ref))

    shapes = (((4, rows, 4 * LANES + BLOCK), bf16),) * 2
    arrays = (scalars, qkv, proj, wide, narrow, gains)
    return kernel_call(kernel, "pack", shapes, arrays, limit=16)


def settle(scalars, parts):
    rows, width = parts[0].shape[1:]
    total = TEAM * rows
    spare = UNITS % LANES

    def kernel(scalar_ref, *refs):
        heads_ref, beside_ref, feed_ref = refs[4:]
        lane = lax.broadcasted_iota(jnp.int32, (16, LANES), 1)
        line = lax.broadcasted_iota(jnp.int32, (16, LANES), 0)
        gains = jnp.zeros((16, LANES), f32)
        for place in range(TEAM):
            ref, side = refs[place % 4], place // 4
            owner = token_block(scalar_ref, place)
            here = pl.ds(pl.multiple_of(owner * rows, rows), rows)
            heads_ref[here, :] = ref[side, :, : 3 * LANES]
            beside_ref[here, :] = ref[side, :, 3 * LANES : 4 * LANES]
            feed_ref[here, :] = ref[side, :, 4 * LANES :]
            first = owner * rows
            tile = ref[side, :, 4 * LANES + SPAN - LANES : 4 * LANES + SPAN].astype(f32)
            at = first % LANES
            tile = pltpu.roll(tile, (at + LANES - spare) % LANES, 1)
            own = (lane >= at) & (lane < at + rows)
            for i in range(2):
                wanted = own & (line == 2 * i + first // LANES)
                gains += jnp.where(wanted, tile[i : i + 1, :], 0.0)
        beside_ref[total:, :] = gains.astype(bf16)

    shapes = (
        ((total, 3 * LANES), bf16),
        ((total + 16, LANES), bf16),
        ((total, width - 4 * LANES), bf16),
    )
    return kernel_call(kernel, "settle", shapes, (scalars, *parts), limit=12)


def edges(parts, scalars, blocks):
    rows = parts.shape[0] // TEAM

    def kernel(scalar_ref, part_ref, first_ref, last_ref):
        core, chip = scalar_ref[0] % 2, scalar_ref[0] // 2
        for out, at, offset in ((first_ref, core * 4 + chip, 0), (last_ref, (1 - core) * 4 + (3 ^ chip), rows - HALF)):
            here = pl.ds(pl.multiple_of(at * rows + offset, HALF), HALF)
            for tile in range(D // LANES):
                part = permuted_tile(part_ref, here, tile, scalar_ref[1], D // blocks)
                out[:, tile * LANES : (tile + 1) * LANES] = part.astype(out.dtype)

    return kernel_call(kernel, "edges", (((HALF, D), bf16),) * 2, (scalars, parts), limit=8)


def turn(value):
    lane = lax.broadcasted_iota(jnp.int32, value.shape, 1)
    first = (lane % HEAD_DIM) < HEAD_DIM // 2
    ahead = pltpu.roll(value, LANES - HEAD_DIM // 2, 1)
    behind = pltpu.roll(value, HEAD_DIM // 2, 1)
    return jnp.where(first, -ahead, behind)


def only_head(value, head):
    lane = lax.broadcasted_iota(jnp.int32, value.shape, 1)
    return jnp.where((lane // HEAD_DIM) == head, value, jnp.zeros_like(value))


def stack(scalars, parts):
    rows = parts[0].shape[0]

    def kernel(scalar_ref, *refs):
        for place in range(TEAM):
            refs[TEAM][place * rows : (place + 1) * rows, :] = refs[place][...]

    shapes = (((TEAM * rows, D), bf16),)
    return kernel_call(kernel, "stack", shapes, (scalars, *parts), limit=8)[0]


def attend(scalars, parts, before, behind, gain, weight, cosine, sine, seg_col, seg_row):
    count = parts.shape[0]
    rows = count // TEAM
    block = 2 * HALF

    def kernel(scalar_ref, *refs):
        part_ref, refs = refs[0], refs[1:]
        before_ref, behind_ref, gain_ref, weight_ref = refs[:4]
        cos_ref, sin_ref, seg_col_ref, seg_row_ref = refs[4:8]
        far_refs, out_ref = refs[8:13], refs[13]
        normed_ref, q_ref, k_ref, v_ref, probs_ref, sems = refs[14:]
        gain = gain_ref[...]

        def project(values, place, inner):
            values = values.astype(f32)
            centre = values - jnp.mean(values, axis=1, keepdims=True)
            spread = jnp.mean(centre * centre, axis=1, keepdims=True)
            normed = (centre * lax.rsqrt(spread + norm_eps) * gain).astype(bf16)
            both = dot(normed, weight_ref[...])
            cosine, sine = cos_ref[place, :], sin_ref[place, :]
            turned = lambda u: (u * cosine + turn(u) * sine).astype(bf16)
            k_ref[place, :] = turned(both[:, LANES : 2 * LANES])
            v_ref[place, :] = both[:, 2 * LANES :].astype(bf16)
            if inner is not None:
                normed_ref[inner, :] = normed
                q_ref[inner, :] = turned(both[:, :LANES])

        for place in range(TEAM):
            project(
                part_ref[place * rows : (place + 1) * rows, :],
                block_rows(scalar_ref, place, rows, HALF),
                block_rows(scalar_ref, place, rows),
            )
        project(before_ref[...], slice(0, HALF), None)
        project(behind_ref[...], slice(count + HALF, count + 2 * HALF), None)

        copies = [
            pltpu.make_async_copy(ref, far_ref, sems.at[i])
            for i, (ref, far_ref) in enumerate(
                zip((normed_ref, q_ref, k_ref, v_ref), far_refs)
            )
        ]
        for copy in copies:
            copy.start()
        line = lax.broadcasted_iota(jnp.int32, (block, 2 * block), 0)
        column = lax.broadcasted_iota(jnp.int32, (block, 2 * block), 1)
        window = jnp.abs(line + HALF - column) <= HALF
        lane = lax.broadcasted_iota(jnp.int32, (block, LANES), 1)
        for first in range(0, count, block):
            allowed = window & (
                seg_col_ref[first + HALF : first + HALF + block, :]
                == seg_row_ref[:, first : first + 2 * block]
            )
            query_low = q_ref[first : first + block, :]
            key_low = k_ref[first : first + 2 * block, :]
            value_low = v_ref[first : first + 2 * block, :]
            results = []
            for head in range(2):
                scores = dot_rt(only_head(query_low, head), key_low) * score_scale
                scores = jnp.where(allowed, scores, -1e30)
                top = jnp.max(scores, axis=1, keepdims=True)
                raised = jnp.where(allowed, jnp.exp(scores - top), 0.0)
                probs = raised / jnp.sum(raised, axis=1, keepdims=True)
                probs = probs.astype(bf16)
                probs_ref[head, first : first + block, :] = probs
                results.append(dot(probs, value_low))
            out_ref[first : first + block, :] = jnp.where(
                lane < HEAD_DIM, results[0], results[1]
            ).astype(bf16)
            copies.append(
                pltpu.make_async_copy(
                    probs_ref.at[:, pl.ds(first, block), :],
                    far_refs[4].at[:, pl.ds(first, block), :],
                    sems.at[4 + first // block],
                )
            )
            copies[-1].start()
        for copy in copies:
            copy.wait()

    shapes = (
        ((count, D), bf16),
        ((count, LANES), bf16),
        ((count + 2 * HALF, LANES), bf16),
        ((count + 2 * HALF, LANES), bf16),
        ((2, count, 4 * HALF), bf16),
        ((count, LANES), bf16),
    )
    arrays = (scalars, parts, before, behind, gain, weight, cosine, sine, seg_col, seg_row)
    scratch = [pltpu.VMEM(*shape) for shape in shapes[:5]]
    scratch.append(pltpu.SemaphoreType.DMA((4 + count // block,)))
    return kernel_call(kernel, "attend", shapes, arrays, scratch, 24, 5)


def mix(scalars, inputs, attended, projs, gain):
    count = inputs.shape[0]
    rows = count // TEAM

    def kernel(scalar_ref, x_ref, *refs):
        a_refs, w_refs = [refs[i * TEAM : (i + 1) * TEAM] for i in range(2)]
        gain_ref, n_ref, own_ref, proj_ref = refs[2 * TEAM :]
        for j in range(TEAM):
            proj_ref[:, j * LANES : (j + 1) * LANES] = w_refs[j][...]
        for place in range(0, TEAM, 2):
            pair = (place, place + 1)
            here = slice(place * rows, (place + 2) * rows)
            attended = jnp.concatenate(
                [
                    jnp.concatenate([ref[block_rows(scalar_ref, i, rows), :] for ref in a_refs], axis=1)
                    for i in pair
                ],
                axis=0,
            )
            middle = x_ref[here, :].astype(f32) + dot_rt(attended, proj_ref[...])
            if place == 0:
                own_ref[...] = middle[:rows]
            centre = middle - jnp.mean(middle, axis=1, keepdims=True)
            spread = jnp.mean(centre * centre, axis=1, keepdims=True)
            n_ref[here, :] = (centre * lax.rsqrt(spread + norm_eps) * gain_ref[...]).astype(bf16)

    shapes = (((count, D), bf16), ((rows, D), f32))
    arrays = (scalars, inputs, *attended, *projs, gain)
    return kernel_call(kernel, "mix", shapes, arrays, (pltpu.VMEM((D, D), bf16),), 20)


def feed_forward(scalars, normed, grads, weight):
    count = normed.shape[0]
    rows = count // TEAM

    def kernel(scalar_ref, n_ref, o_ref, w_ref, i_ref, t_ref, p_ref, keep_ref, give_ref):
        for place in (4, 6, 0, 2):
            here = slice(place * rows, (place + 2) * rows)
            out_low = o_ref[here, :]
            normed = n_ref[here, :]
            inner = dot(normed, w_ref[:, :SPAN])
            gate = dot(normed, w_ref[:, SPAN : 2 * SPAN])
            product_grad = dot(out_low, w_ref[:, 2 * SPAN :])
            below = 0.5 * (1.0 + lax.erf(inner * 0.7071067811865476))
            active = inner * below
            slope = below + inner * (jnp.exp(-0.5 * inner * inner) * 0.3989422804014327)
            p_ref[here, :] = (active * gate).astype(bf16)
            inner_grad = (product_grad * gate * slope).astype(bf16)
            gate_grad = (product_grad * active).astype(bf16)
            i_ref[here, :] = inner_grad
            t_ref[here, :] = gate_grad
            back = dot_rt(inner_grad, w_ref[:, :SPAN]) + dot_rt(gate_grad, w_ref[:, SPAN : 2 * SPAN])
            if place < 4:
                keep_ref[here, :] = back
            else:
                give_ref[(place - 4) * rows : (place - 2) * rows, :] = back.astype(bf16)

    shapes = (
        ((count, SPAN), bf16),
        ((count, SPAN), bf16),
        ((count, SPAN), bf16),
        ((count // 2, D), f32),
        ((count // 2, D), bf16),
    )
    arrays = (scalars, normed, grads, weight)
    return kernel_call(kernel, "feed_forward", shapes, arrays, (), 20)


def divided(block, bit):
    return (block >> bit) & 1, (block & ((1 << bit) - 1)) | ((block >> (bit + 1)) << bit)


def feed_grads(scalars, normed, grads, inner_grad, gate_grad, product, blocks):
    size = D // (2 * blocks)

    def kernel(scalar_ref, n_ref, o_ref, i_ref, t_ref, p_ref, *outs):
        for number in range(2 * blocks):
            columns = slice(number * size, (number + 1) * size)
            side, at = divided(number // 2, 0)
            ref, here = outs[2 * (number % 2) + side], slice(at * size, (at + 1) * size)
            grad = o_ref[:, columns]
            normed = n_ref[:, columns]
            ref[here, :SPAN] = dot_lt(normed, i_ref[...]).astype(bf16)
            ref[here, SPAN : 2 * SPAN] = dot_lt(normed, t_ref[...]).astype(bf16)
            ref[here, 2 * SPAN :] = dot_lt(grad, p_ref[...]).astype(bf16)

    shapes = (((D // 4, BLOCK), bf16),) * 4
    arrays = (scalars, normed, grads, inner_grad, gate_grad, product)
    outs = kernel_call(kernel, "feed_grads", shapes, arrays, limit=18)
    return (outs[:2], outs[2:])


def attend_back(scalars, parts, proj, probs, query, key, value, cosine, sine):
    rows = parts[0].shape[0]
    count, extended = query.shape[0], key.shape[0]
    block = 2 * HALF

    def kernel(scalar_ref, *refs):
        part_refs, refs = refs[:TEAM], refs[TEAM:]
        proj_ref, probs_ref, q_ref, k_ref, v_ref, cos_ref, sin_ref = refs[:7]
        out_ref, edge_ref, first_ref, last_ref, grad_ref, dk_ref, dv_ref = refs[7:]
        for place in range(0, TEAM, 2):
            both = jnp.concatenate([part_refs[place][...], part_refs[place + 1][...]], axis=0)
            both = dot(both, proj_ref[...]).astype(bf16)
            grad_ref[block_rows(scalar_ref, place, rows), :] = both[:rows]
            grad_ref[block_rows(scalar_ref, place + 1, rows), :] = both[rows:]
        lane = lax.broadcasted_iota(jnp.int32, (block, LANES), 1)
        dk_ref[...] = jnp.zeros_like(dk_ref)
        dv_ref[...] = jnp.zeros_like(dv_ref)
        for first in range(0, count, block):
            grad = grad_ref[first : first + block, :]
            query_low = q_ref[first : first + block, :]
            key_low = k_ref[first : first + 2 * block, :]
            value_low = v_ref[first : first + 2 * block, :]
            results = []
            key_sum = jnp.zeros((2 * block, LANES), f32)
            value_sum = jnp.zeros((2 * block, LANES), f32)
            for head in range(2):
                own_grad = only_head(grad, head)
                probs_low = probs_ref[head, first : first + block, :]
                probs = probs_low.astype(f32)
                probs_grad = dot_rt(own_grad, value_low)
                delta = jnp.sum(probs * probs_grad, axis=1, keepdims=True)
                scores_grad = (probs * (probs_grad - delta)).astype(bf16)
                results.append(dot(scores_grad, key_low))
                key_sum += dot_lt(scores_grad, only_head(query_low, head))
                value_sum += dot_lt(probs_low, own_grad)
            dk_ref[first : first + 2 * block, :] += key_sum * score_scale
            dv_ref[first : first + 2 * block, :] += value_sum
            query_grad = jnp.where(lane < HEAD_DIM, results[0], results[1]) * score_scale
            place = slice(first + HALF, first + HALF + block)
            out_ref[first : first + block, :LANES] = (
                query_grad * cos_ref[place, :] - turn(query_grad * sin_ref[place, :])
            ).astype(bf16)
        inner = slice(HALF, HALF + count)
        out_ref[:, LANES : 2 * LANES] = turned_back(dk_ref[inner, :], cos_ref, sin_ref, inner)
        out_ref[:, 2 * LANES :] = dv_ref[inner, :].astype(bf16)
        for i, place in enumerate((HALF, count)):
            edge_ref[i, :, :LANES] = dk_ref[place : place + HALF, :]
            edge_ref[i, :, LANES:] = dv_ref[place : place + HALF, :]
        for out, edge in ((first_ref, slice(0, HALF)), (last_ref, slice(extended - HALF, extended))):
            out[:, :LANES] = dk_ref[edge, :].astype(bf16)
            out[:, LANES:] = dv_ref[edge, :].astype(bf16)

    shapes = (
        ((count, 3 * LANES), bf16),
        ((2, HALF, 2 * LANES), f32),
        ((HALF, 2 * LANES), bf16),
        ((HALF, 2 * LANES), bf16),
    )
    arrays = (scalars, *parts, proj, probs, query, key, value, cosine, sine)
    scratch = (
        pltpu.VMEM((count, LANES), bf16),
        pltpu.VMEM((extended, LANES), f32),
        pltpu.VMEM((extended, LANES), f32),
    )
    return kernel_call(kernel, "attend_back", shapes, arrays, scratch, 18)


def turned_back(grad, cos_ref, sin_ref, place):
    return (grad * cos_ref[place, :] - turn(grad * sin_ref[place, :])).astype(bf16)


def join(scalars, grads, edge, before, behind, cosine, sine, rows):
    count = grads.shape[0]

    def kernel(scalar_ref, in_ref, edge_ref, before_ref, behind_ref, cos_ref, sin_ref, out_ref, team_ref):
        out_ref[...] = in_ref[...]
        for i, (ref, first) in enumerate(((before_ref, 0), (behind_ref, count - HALF))):
            total = edge_ref[i] + ref[...].astype(f32)
            here, place = slice(first, first + HALF), slice(first + HALF, first + 2 * HALF)
            out_ref[here, LANES : 2 * LANES] = turned_back(
                total[:, :LANES], cos_ref, sin_ref, place
            )
            out_ref[here, 2 * LANES :] = total[:, LANES:].astype(bf16)
        for place in range(TEAM):
            team_ref[place * rows : (place + 1) * rows, :] = out_ref[
                block_rows(scalar_ref, place, rows), :
            ]

    shapes = (((count, 3 * LANES), bf16),) * 2
    arrays = (scalars, grads, edge, before, behind, cosine, sine)
    return kernel_call(kernel, "join_halo", shapes, arrays, limit=10)


def head_grads(scalars, parts, normed, grads, attended, blocks):
    rows = parts[0].shape[0]
    size = D // blocks

    def kernel(scalar_ref, *refs):
        part_refs, refs = refs[:TEAM], refs[TEAM:]
        n_ref, g_ref, a_ref, keep_ref, give_ref, middle_ref, beside_ref = refs
        for place in range(TEAM):
            here = slice(place * rows, (place + 1) * rows)
            middle_ref[here, :] = part_refs[place][...]
            beside_ref[here, :] = a_ref[block_rows(scalar_ref, place, rows), :]
        for block in range(blocks):
            columns = slice(block * size, (block + 1) * size)
            side, at = divided(block, 0)
            ref, here = (keep_ref, give_ref)[side], slice(at * size, (at + 1) * size)
            ref[here, : 3 * LANES] = dot_lt(n_ref[:, columns], g_ref[...]).astype(bf16)
            ref[here, 3 * LANES :] = dot_lt(middle_ref[:, columns], beside_ref[...]).astype(bf16)

    count = TEAM * rows
    shapes = (((D // 2, 4 * LANES), bf16),) * 2
    scratch = (pltpu.VMEM((count, D), bf16), pltpu.VMEM((count, LANES), bf16))
    arrays = (scalars, *parts, normed, grads, attended)
    return kernel_call(kernel, "head_grads", shapes, arrays, scratch, 18)


def token_layout(first_token, count, total_tokens, document_starts):
    seq_length = total_tokens // document_starts.shape[0]
    global_ids = first_token + jnp.arange(count, dtype=jnp.int32)
    in_range = (global_ids >= 0) & (global_ids < total_tokens)
    safe_ids = jnp.clip(global_ids, 0, total_tokens - 1)
    sequence = safe_ids // seq_length
    place = safe_ids % seq_length
    starts = jnp.take(document_starts, sequence, axis=0)
    passed = starts <= place[:, None]
    segment = sequence * (document_starts.shape[1] + 1) + jnp.sum(passed.astype(jnp.int32), axis=1)
    segment = jnp.where(in_range, segment, -1)
    doc_place = place - jnp.max(jnp.where(passed, starts, 0), axis=1)
    return (segment, doc_place)


def rope_tables(doc_place):
    freq = rope_base ** (-(2.0 * jnp.arange(HEAD_DIM // 2, dtype=f32)) / HEAD_DIM)
    angles = doc_place.astype(f32)[:, None] * freq[None, :]
    spread = lambda table: jnp.tile(table, (1, LANES * 2 // HEAD_DIM))
    return (spread(jnp.cos(angles)), spread(jnp.sin(angles)))


def norm_parts(values):
    centre = values - jnp.mean(values, axis=-1, keepdims=True)
    spread = jnp.mean(centre * centre, axis=-1, keepdims=True)
    root = lax.rsqrt(spread + norm_eps)
    return (centre * root, root)


def norm_back(grad, gain, hat, root):
    scaled = grad * gain
    return root * (
        scaled
        - jnp.mean(scaled, axis=-1, keepdims=True)
        - hat * jnp.mean(scaled * hat, axis=-1, keepdims=True)
    )


def on_device(
    layer_input,
    qkv_weight,
    proj_weight,
    wide_weight,
    narrow_weight,
    first_gain,
    second_gain,
    output_grad,
    document_starts,
):
    size = lax.axis_size("dp")
    chips = size // 2
    bits = chips.bit_length() - 1
    far = tuple(range(2, bits))[::-1]
    device = lax.axis_index("dp").astype(jnp.int32)
    chip, core, member = device // 2, device % 2, device % TEAM
    near_key, far_key = chip % 4, chip - chip % 4
    is_first = core == 0
    rows = layer_input.shape[0]
    tokens = TEAM * rows
    own_rows = qkv_weight.shape[0]
    team_rows = TEAM * own_rows

    def to_team(parts):
        return [parts[0]] + [swap(parts[j], 2 * j) for j in (1, 2, 3)]

    def gather_team(value):
        near = to_team([value] * 4)
        return near + [swap(part, 1) for part in near]

    def both_sides(near):
        return near + [swap(part, 1) for part in near]

    def scatter_team(keeps, gives):
        got = swap(jnp.concatenate(gives, axis=0), 1)
        near = [
            jnp.concatenate(
                [
                    keep[j * rows : (j + 1) * rows]
                    + got[(4 * i + j) * rows : (4 * i + j + 1) * rows].astype(f32)
                    for i, keep in enumerate(keeps)
                ],
                axis=0,
            )
            for j in range(4)
        ]
        parts = [near[0]] + [part.astype(bf16) for part in near[1:]]
        got = to_team(parts)
        total = (got[0] + got[1].astype(f32)) + (got[2].astype(f32) + got[3].astype(f32))
        return total, got[1], parts[1]

    def deal_back(value):
        width = value.shape[1]
        value = value.astype(bf16).reshape(2, 2, 2 * own_rows, width)
        value = turned_by(value, near_key, (0, 1)).reshape(4, 2 * own_rows, width)
        parts = to_team([value[j] for j in range(4)])
        landed = parts[1]
        value = jnp.stack(parts, axis=0)
        value = turned_by(value.reshape(2, 2, 2, own_rows, width), core, (2,))
        value = jnp.stack([value[:, :, 0], swap(value[:, :, 1], 1)], axis=2)
        value = turned_by(value, member, (0, 1, 2)).astype(f32).reshape(TEAM, own_rows, width)
        return value, landed

    scalars = jnp.stack([member, far_key])
    zones = D // team_rows

    mine, give = pack(
        scalars, qkv_weight, proj_weight.T, wide_weight,
        jnp.pad(narrow_weight.T, ((0, 0), (0, -FF % LANES))),
        jnp.pad(
            jnp.stack([first_gain, second_gain]).astype(f32),
            ((0, 0), (UNITS, SPAN - UNITS - own_rows)),
        ),
    )
    both = jnp.stack([mine, swap(give, 1)], axis=1)
    parts = to_team([both[j] for j in range(4)])
    landed = parts[1]
    if own_rows % 16 == 0:
        head_rows, beside_rows, unit_rows = settle(scalars, parts)
    else:
        dealt = jnp.stack(parts, axis=0).reshape(2, 2, 2, own_rows, -1)
        dealt = turned_by(dealt, member, (0, 1, 2)).reshape(TEAM, own_rows, -1)
        at = 4 * LANES + UNITS
        gains = [dealt[:, i, at : at + own_rows].reshape(-1) for i in range(2)]
        gains = [jnp.pad(gain, (0, 2 * LANES - team_rows)).reshape(2, LANES) for gain in gains]
        dealt = dealt.reshape(team_rows, -1)
        head_rows, unit_rows = dealt[:, : 3 * LANES], dealt[:, 4 * LANES :]
        beside_rows = jnp.concatenate(
            [dealt[:, 3 * LANES : 4 * LANES], *gains, jnp.zeros((12, LANES), bf16)], axis=0
        )

    own_input = reorder(after(layer_input, parts), far_key, chips)
    inputs = gather_team(own_input)
    team_input = stack(scalars, inputs)
    team_first, team_last = edges(team_input, scalars, chips)
    before, behind = shifted(team_last, 1), shifted(team_first, -1)

    stages = []
    beside = gather_rows(beside_rows, far, 2, bits).reshape(zones, team_rows + 16, LANES)
    head_w = gather_rows(head_rows, far, 2, bits, None, stages)
    proj_w = beside[:, :team_rows].reshape(D, LANES)
    gain_one, gain_two = [
        beside[:, team_rows + i : team_rows + i + 2]
        .reshape(zones, -1)[:, :team_rows]
        .reshape(1, D)
        .astype(f32)
        for i in (0, 2)
    ]
    projs = to_team([proj_w] * 4)

    grad_late = after(output_grad, parts)
    out_grad = reorder(grad_late, far_key, chips)
    grads_low = to_team(
        [after(reorder(grad_late.astype(bf16), far_key, chips), inputs[3])] * 4
    )

    before, behind = reorder(before, far_key, chips), reorder(behind, far_key, chips)
    places = after(document_starts, both)
    segment, doc_place = token_layout(
        device // TEAM * tokens - HALF, tokens + 2 * HALF, rows * size, places
    )
    cosine, sine = rope_tables(doc_place)
    normed_low, query_low, key_low, value_low, probs, attended_low = attend(
        scalars, team_input, before, behind, gain_one, head_w, cosine, sine,
        segment[:, None], segment[None, :],
    )
    attended = gather_team(attended_low)
    projs = both_sides(after(projs, attended_low))
    out_low = stack(scalars, both_sides(after(grads_low, attended_low)))

    feed_w = gather_rows(after(unit_rows, stages[0]), far, 2, bits, (attended_low, head_w))
    normed_two, middle_own = mix(scalars, team_input, attended, projs, gain_two)
    inner_grad, gate_grad, product, keep, give = feed_forward(
        scalars, normed_two, out_low, feed_w
    )
    wide_back, landed, sent = scatter_team([keep], [give])
    feed_halves = feed_grads(
        scalars, after(normed_two, sent), out_low, inner_grad, gate_grad, product, zones
    )

    hat_own, root_own = norm_parts(middle_own)
    middle_grad = out_grad + norm_back(wide_back, gain_two, hat_own, root_own)
    middle = gather_team(after(middle_grad.astype(bf16), feed_halves))
    feed_got = [
        after(scatter_first(feed_halves[0], far), middle[1]),
        scatter_first(after(feed_halves[1], middle[1]), far),
    ]
    feed_half = [scatter_second(*pair) for pair in zip(feed_halves, feed_got)]
    own_grads, edge_grads, rim_first, rim_last = attend_back(
        after(scalars, feed_half[0]), middle, proj_w, probs, query_low, key_low, value_low, cosine, sine
    )
    from_before, from_behind = shifted(rim_last, 1), shifted(rim_first, -1)
    grads, team_grads = join(
        after(scalars, feed_half[1]), own_grads, edge_grads, from_before, from_behind, cosine, sine, rows
    )
    halves = head_grads(scalars, middle, normed_low, grads, attended_low, zones)
    late_product, team_grads = after((product, team_grads), halves)
    narrow_w = feed_w[:, 2 * SPAN :]
    half = tokens // 2
    back_sums, landed, sent = scatter_team(
        [dot_rt(team_grads[:half], head_w), dot_rt(late_product[:half], narrow_w)],
        [
            dot_rt(team_grads[half:], head_w).astype(bf16),
            dot_rt(late_product[half:], narrow_w).astype(bf16),
        ],
    )
    out_sum = back_sums[rows:]
    feed_first, feed_second = [
        scatter_rows(half, far, 2, bits, (back_sums,)) for half in feed_half
    ]
    feed_sums = jnp.concatenate([feed_first, feed_second], axis=0)
    first_back, late_sums = after((back_sums[:rows], feed_sums), feed_sums, landed)
    feed_shares, feed_landed = deal_back(late_sums)
    got = after(scatter_first(halves, far), landed)
    head_sums = scatter_rows(scatter_second(halves, got), far, 2, bits)
    hat_own, root_own = norm_parts(own_input.astype(f32))
    input_grad = reorder(
        middle_grad + norm_back(first_back, gain_one, hat_own, root_own), far_key, chips
    )
    layer_output = reorder((middle_own + out_sum).astype(bf16), far_key, chips)

    inner_share, gate_share, narrow_share = [
        feed_shares[:, :, i * SPAN : i * SPAN + UNITS].transpose(1, 0, 2).reshape(own_rows, FF)
        for i in range(3)
    ]
    wide_share = jnp.concatenate([inner_share, gate_share], axis=1)
    head_shares, landed = deal_back(after(head_sums, feed_landed))
    query_share, key_share, value_share, proj_share = [
        head_shares[:, :, i * LANES : (i + 1) * LANES].transpose(1, 0, 2).reshape(own_rows, D)
        for i in range(4)
    ]
    qkv_share = jnp.concatenate([query_share, key_share, value_share], axis=1)

    gain_one_share = jnp.sum(qkv_weight.astype(f32) * qkv_share, axis=1) / first_gain.astype(f32)
    gain_two_share = jnp.sum(wide_weight.astype(f32) * wide_share, axis=1) / second_gain.astype(f32)
    return (
        layer_output,
        input_grad,
        qkv_share,
        proj_share.T,
        wide_share,
        narrow_share.T,
        gain_one_share,
        gain_two_share,
    )


def solution(mesh):
    placed = (
        P("dp", None),
        P("dp", None),
        P(None, "dp"),
        P("dp", None),
        P(None, "dp"),
        P("dp"),
        P("dp"),
        P("dp", None),
        P(),
    )
    return jax.shard_map(
        on_device,
        mesh=mesh,
        in_specs=placed,
        out_specs=(
            P("dp", None),
            P("dp", None),
            P("dp", None),
            P(None, "dp"),
            P("dp", None),
            P(None, "dp"),
            P("dp"),
            P("dp"),
        ),
        check_vma=False,
    )
```

```python
import jax
import jax.numpy as jnp
from jax import lax
from jax.experimental import pallas as pl
from jax.experimental.pallas import tpu as pltpu
from jax.sharding import PartitionSpec as P

D = 1024
HEADS = 16
HEAD_DIM = 64
FF = 2624
HALF = 64
LANES = 128

norm_eps = 1e-05
rope_base = 10000.0
score_scale = HEAD_DIM ** (-0.5)

TEAM = 8
UNITS = FF // TEAM
SPAN = -(-UNITS // LANES) * LANES
BLOCK = 3 * SPAN

bf16 = jnp.bfloat16
f32 = jnp.float32


def dot(left, right):
    return lax.dot_general(left, right, (((1,), (0,)), ((), ())), preferred_element_type=f32)


def dot_rt(left, right):
    return lax.dot_general(left, right, (((1,), (1,)), ((), ())), preferred_element_type=f32)


def dot_lt(left, right):
    return lax.dot_general(left, right, (((0,), (0,)), ((), ())), preferred_element_type=f32)


def swap(value, bit):
    size = lax.axis_size("dp")
    return lax.ppermute(value, "dp", [(i, i ^ bit) for i in range(size)])


def shifted(value, step):
    size = lax.axis_size("dp")
    pairs = [(i, i + TEAM * step) for i in range(size) if 0 <= i + TEAM * step < size]
    return lax.ppermute(value, "dp", pairs)


def after(value, *others):
    return lax.optimization_barrier((value, *others))[0]


def gather_rows(value, order, low, high, gate=None, stages=None):
    rows, columns = value.shape
    value = value.reshape((1,) * (high - low) + (rows, columns))
    for bit in order:
        other = swap(value, 2 << bit)
        if gate is not None and bit == order[0]:
            other = after(other, *gate)
        value = jnp.concatenate([value, other], axis=high - 1 - bit)
        if stages is not None:
            stages.append(value)
    return value.reshape(-1, columns)


def scatter_first(halves, order):
    return swap(halves[1], 2 << order[-1])


def scatter_second(halves, got):
    return (halves[0].astype(f32) + got.astype(f32)).astype(bf16)


def scatter_rows(value, order, low, high, gates=()):
    order = order[::-1]
    left = [bit for bit in range(high - 1, low - 1, -1) if bit != order[0]]
    rows, columns = value.shape[0] >> len(left), value.shape[1]
    value = value.reshape((2,) * len(left) + (rows, columns))
    for bit in order[1:]:
        value = value.astype(bf16)
        axis = left.index(bit)
        keep = lax.slice_in_dim(value, 0, 1, axis=axis)
        give = lax.slice_in_dim(value, 1, 2, axis=axis)
        got = swap(give, 2 << bit)
        if bit == order[-1] and gates:
            got = after(got, *gates)
        value = keep.astype(f32) + got.astype(f32)
    return value.reshape(rows, columns)


def turned_by(value, key, axes):
    for place, axis in enumerate(axes[::-1]):
        value = jnp.where((key >> place) % 2 == 1, jnp.flip(value, axis), value)
    return value


def permuted_tile(ref, rows, tile, key, block):
    per_tile = max(LANES // block, 1)
    if block >= LANES:
        source = jnp.bitwise_xor(key * (block // LANES), tile)
    else:
        source = jnp.bitwise_xor(key // per_tile, tile)
    part = ref[rows, pl.ds(pl.multiple_of(source * LANES, LANES), LANES)].astype(f32)
    lane = lax.broadcasted_iota(jnp.int32, part.shape, 1)
    step, place = block, 1
    while step < LANES:
        up = pltpu.roll(part, step, 1)
        down = pltpu.roll(part, LANES - step, 1)
        part = jnp.where((key // place) % 2 == 1, jnp.where((lane & step) != 0, up, down), part)
        step, place = step * 2, place * 2
    return part


def reorder(value, key, blocks, stacked=False):
    rows, width = value.shape

    def kernel(key_ref, in_ref, out_ref):
        for tile in range(width // LANES):
            part = permuted_tile(in_ref, slice(None), tile, key_ref[0], width // blocks)
            part = part.astype(out_ref.dtype)
            if stacked:
                out_ref[tile * rows : (tile + 1) * rows, :] = part
            else:
                out_ref[:, tile * LANES : (tile + 1) * LANES] = part

    shape = (rows * width // LANES, LANES) if stacked else value.shape
    return pl.pallas_call(
        kernel,
        out_shape=jax.ShapeDtypeStruct(shape, value.dtype),
        in_specs=[
            pl.BlockSpec(memory_space=pltpu.SMEM),
            pl.BlockSpec(memory_space=pltpu.VMEM),
        ],
        out_specs=pl.BlockSpec(memory_space=pltpu.VMEM),
        name="reorder",
        compiler_params=pltpu.CompilerParams(vmem_limit_bytes=8 * 2**20),
    )(key.reshape(1), value)


def kernel_call(kernel, name, shapes, arrays, scratch=(), limit=32, far_out=0):
    space = lambda place: pl.BlockSpec(memory_space=place)
    return pl.pallas_call(
        kernel,
        out_shape=tuple(jax.ShapeDtypeStruct(*shape) for shape in shapes),
        in_specs=[space(pltpu.SMEM)] + [space(pltpu.VMEM)] * (len(arrays) - 1),
        out_specs=(space(pltpu.HBM),) * far_out + (space(pltpu.VMEM),) * (len(shapes) - far_out),
        scratch_shapes=list(scratch),
        name=name,
        compiler_params=pltpu.CompilerParams(vmem_limit_bytes=limit * 2**20),
    )(*arrays)


def token_block(member_ref, place):
    core, chip = member_ref[0] % 2, member_ref[0] // 2
    return ((place % 4) ^ chip) * 2 + ((place // 4) ^ core)


def block_rows(member_ref, place, rows, offset=0):
    at = token_block(member_ref, place) * rows + offset
    return pl.ds(pl.multiple_of(at, min(rows, HALF)), rows)


def pack(scalars, qkv, proj, wide, narrow, gains):
    rows = qkv.shape[0]

    def kernel(scalar_ref, qkv_ref, proj_ref, wide_ref, narrow_ref, gain_ref, mine_ref, give_ref):
        core, chip = scalar_ref[0] % 2, scalar_ref[0] // 2
        lane = lax.broadcasted_iota(jnp.int32, (rows, SPAN), 1)

        def units(ref, start):
            base = start // LANES * LANES
            window = -(-(start - base + UNITS) // LANES) * LANES
            part = ref[:, base : base + window].astype(f32)
            if start > base:
                part = pltpu.roll(part, window - (start - base), 1)
            return jnp.where(lane < UNITS, part[:, :SPAN], 0.0)

        for owner in range(TEAM):
            place = (owner // 2) ^ chip

            def write(ref):
                for i in range(3):
                    at = i * D + owner * LANES
                    ref[place, :, i * LANES : (i + 1) * LANES] = qkv_ref[:, at : at + LANES]
                ref[place, :, 3 * LANES : 4 * LANES] = proj_ref[
                    :, owner * LANES : (owner + 1) * LANES
                ]
                inner = units(wide_ref, owner * UNITS)
                for i in range(2):
                    line = lax.broadcasted_iota(jnp.int32, (rows, SPAN), 0)
                    inner = jnp.where((lane >= UNITS) & (line == i), gain_ref[i : i + 1, :], inner)
                gate = units(wide_ref, FF + owner * UNITS)
                out = units(narrow_ref, owner * UNITS)
                for i, value in enumerate((inner, gate, out)):
                    at = 4 * LANES + i * SPAN
                    ref[place, :, at : at + SPAN] = value.astype(bf16)

            pl.when(core == owner % 2)(lambda: write(mine_ref))
            pl.when(core != owner % 2)(lambda: write(give_ref))

    shapes = (((4, rows, 4 * LANES + BLOCK), bf16),) * 2
    arrays = (scalars, qkv, proj, wide, narrow, gains)
    return kernel_call(kernel, "pack", shapes, arrays, limit=16)


def settle(scalars, parts):
    rows, width = parts[0].shape[1:]
    total = TEAM * rows
    spare = UNITS % LANES

    def kernel(scalar_ref, *refs):
        heads_ref, beside_ref, feed_ref = refs[4:]
        lane = lax.broadcasted_iota(jnp.int32, (16, LANES), 1)
        line = lax.broadcasted_iota(jnp.int32, (16, LANES), 0)
        gains = jnp.zeros((16, LANES), f32)
        for place in range(TEAM):
            ref, side = refs[place % 4], place // 4
            owner = token_block(scalar_ref, place)
            here = pl.ds(pl.multiple_of(owner * rows, rows), rows)
            heads_ref[here, :] = ref[side, :, : 3 * LANES]
            beside_ref[here, :] = ref[side, :, 3 * LANES : 4 * LANES]
            feed_ref[here, :] = ref[side, :, 4 * LANES :]
            first = owner * rows
            tile = ref[side, :, 4 * LANES + SPAN - LANES : 4 * LANES + SPAN].astype(f32)
            at = first % LANES
            tile = pltpu.roll(tile, (at + LANES - spare) % LANES, 1)
            own = (lane >= at) & (lane < at + rows)
            for i in range(2):
                wanted = own & (line == 2 * i + first // LANES)
                gains += jnp.where(wanted, tile[i : i + 1, :], 0.0)
        beside_ref[total:, :] = gains.astype(bf16)

    shapes = (
        ((total, 3 * LANES), bf16),
        ((total + 16, LANES), bf16),
        ((total, width - 4 * LANES), bf16),
    )
    return kernel_call(kernel, "settle", shapes, (scalars, *parts), limit=12)


def edges(parts, scalars, blocks):
    rows = parts.shape[0] // TEAM

    def kernel(scalar_ref, part_ref, first_ref, last_ref):
        core, chip = scalar_ref[0] % 2, scalar_ref[0] // 2
        for out, at, offset in ((first_ref, core * 4 + chip, 0), (last_ref, (1 - core) * 4 + (3 ^ chip), rows - HALF)):
            here = pl.ds(pl.multiple_of(at * rows + offset, HALF), HALF)
            for tile in range(D // LANES):
                part = permuted_tile(part_ref, here, tile, scalar_ref[1], D // blocks)
                out[:, tile * LANES : (tile + 1) * LANES] = part.astype(out.dtype)

    return kernel_call(kernel, "edges", (((HALF, D), bf16),) * 2, (scalars, parts), limit=8)


def turn(value):
    lane = lax.broadcasted_iota(jnp.int32, value.shape, 1)
    first = (lane % HEAD_DIM) < HEAD_DIM // 2
    ahead = pltpu.roll(value, LANES - HEAD_DIM // 2, 1)
    behind = pltpu.roll(value, HEAD_DIM // 2, 1)
    return jnp.where(first, -ahead, behind)


def only_head(value, head):
    lane = lax.broadcasted_iota(jnp.int32, value.shape, 1)
    return jnp.where((lane // HEAD_DIM) == head, value, jnp.zeros_like(value))


def stack(scalars, parts):
    rows = parts[0].shape[0]

    def kernel(scalar_ref, *refs):
        for place in range(TEAM):
            refs[TEAM][place * rows : (place + 1) * rows, :] = refs[place][...]

    shapes = (((TEAM * rows, D), bf16),)
    return kernel_call(kernel, "stack", shapes, (scalars, *parts), limit=8)[0]


def attend(scalars, parts, before, behind, gain, weight, cosine, sine, seg_col, seg_row):
    count = parts.shape[0]
    rows = count // TEAM
    block = 2 * HALF

    def kernel(scalar_ref, *refs):
        part_ref, refs = refs[0], refs[1:]
        before_ref, behind_ref, gain_ref, weight_ref = refs[:4]
        cos_ref, sin_ref, seg_col_ref, seg_row_ref = refs[4:8]
        far_refs, out_ref = refs[8:13], refs[13]
        normed_ref, q_ref, k_ref, v_ref, probs_ref, sems = refs[14:]
        gain = gain_ref[...]

        def project(values, place, inner):
            values = values.astype(f32)
            centre = values - jnp.mean(values, axis=1, keepdims=True)
            spread = jnp.mean(centre * centre, axis=1, keepdims=True)
            normed = (centre * lax.rsqrt(spread + norm_eps) * gain).astype(bf16)
            both = dot(normed, weight_ref[...])
            cosine, sine = cos_ref[place, :], sin_ref[place, :]
            turned = lambda u: (u * cosine + turn(u) * sine).astype(bf16)
            k_ref[place, :] = turned(both[:, LANES : 2 * LANES])
            v_ref[place, :] = both[:, 2 * LANES :].astype(bf16)
            if inner is not None:
                normed_ref[inner, :] = normed
                q_ref[inner, :] = turned(both[:, :LANES])

        for place in range(TEAM):
            project(
                part_ref[place * rows : (place + 1) * rows, :],
                block_rows(scalar_ref, place, rows, HALF),
                block_rows(scalar_ref, place, rows),
            )
        project(before_ref[...], slice(0, HALF), None)
        project(behind_ref[...], slice(count + HALF, count + 2 * HALF), None)

        copies = [
            pltpu.make_async_copy(ref, far_ref, sems.at[i])
            for i, (ref, far_ref) in enumerate(
                zip((normed_ref, q_ref, k_ref, v_ref), far_refs)
            )
        ]
        for copy in copies:
            copy.start()
        line = lax.broadcasted_iota(jnp.int32, (block, 2 * block), 0)
        column = lax.broadcasted_iota(jnp.int32, (block, 2 * block), 1)
        window = jnp.abs(line + HALF - column) <= HALF
        lane = lax.broadcasted_iota(jnp.int32, (block, LANES), 1)
        for first in range(0, count, block):
            allowed = window & (
                seg_col_ref[first + HALF : first + HALF + block, :]
                == seg_row_ref[:, first : first + 2 * block]
            )
            query_low = q_ref[first : first + block, :]
            key_low = k_ref[first : first + 2 * block, :]
            value_low = v_ref[first : first + 2 * block, :]
            results = []
            for head in range(2):
                scores = dot_rt(only_head(query_low, head), key_low) * score_scale
                scores = jnp.where(allowed, scores, -1e30)
                top = jnp.max(scores, axis=1, keepdims=True)
                raised = jnp.where(allowed, jnp.exp(scores - top), 0.0)
                probs = raised / jnp.sum(raised, axis=1, keepdims=True)
                probs = probs.astype(bf16)
                probs_ref[head, first : first + block, :] = probs
                results.append(dot(probs, value_low))
            out_ref[first : first + block, :] = jnp.where(
                lane < HEAD_DIM, results[0], results[1]
            ).astype(bf16)
            copies.append(
                pltpu.make_async_copy(
                    probs_ref.at[:, pl.ds(first, block), :],
                    far_refs[4].at[:, pl.ds(first, block), :],
                    sems.at[4 + first // block],
                )
            )
            copies[-1].start()
        for copy in copies:
            copy.wait()

    shapes = (
        ((count, D), bf16),
        ((count, LANES), bf16),
        ((count + 2 * HALF, LANES), bf16),
        ((count + 2 * HALF, LANES), bf16),
        ((2, count, 4 * HALF), bf16),
        ((count, LANES), bf16),
    )
    arrays = (scalars, parts, before, behind, gain, weight, cosine, sine, seg_col, seg_row)
    scratch = [pltpu.VMEM(*shape) for shape in shapes[:5]]
    scratch.append(pltpu.SemaphoreType.DMA((4 + count // block,)))
    return kernel_call(kernel, "attend", shapes, arrays, scratch, 24, 5)


def mix(scalars, inputs, attended, projs, gain):
    count = inputs.shape[0]
    rows = count // TEAM

    def kernel(scalar_ref, x_ref, *refs):
        a_refs, w_refs = [refs[i * TEAM : (i + 1) * TEAM] for i in range(2)]
        gain_ref, n_ref, own_ref, proj_ref = refs[2 * TEAM :]
        for j in range(TEAM):
            proj_ref[:, j * LANES : (j + 1) * LANES] = w_refs[j][...]
        for place in range(0, TEAM, 2):
            pair = (place, place + 1)
            here = slice(place * rows, (place + 2) * rows)
            attended = jnp.concatenate(
                [
                    jnp.concatenate([ref[block_rows(scalar_ref, i, rows), :] for ref in a_refs], axis=1)
                    for i in pair
                ],
                axis=0,
            )
            middle = x_ref[here, :].astype(f32) + dot_rt(attended, proj_ref[...])
            if place == 0:
                own_ref[...] = middle[:rows]
            centre = middle - jnp.mean(middle, axis=1, keepdims=True)
            spread = jnp.mean(centre * centre, axis=1, keepdims=True)
            n_ref[here, :] = (centre * lax.rsqrt(spread + norm_eps) * gain_ref[...]).astype(bf16)

    shapes = (((count, D), bf16), ((rows, D), f32))
    arrays = (scalars, inputs, *attended, *projs, gain)
    return kernel_call(kernel, "mix", shapes, arrays, (pltpu.VMEM((D, D), bf16),), 20)


def feed_forward(scalars, normed, grads, weight):
    count = normed.shape[0]
    rows = count // TEAM

    def kernel(scalar_ref, n_ref, o_ref, w_ref, i_ref, t_ref, p_ref, keep_ref, give_ref):
        for place in (4, 6, 0, 2):
            here = slice(place * rows, (place + 2) * rows)
            out_low = o_ref[here, :]
            normed = n_ref[here, :]
            inner = dot(normed, w_ref[:, :SPAN])
            gate = dot(normed, w_ref[:, SPAN : 2 * SPAN])
            product_grad = dot(out_low, w_ref[:, 2 * SPAN :])
            below = 0.5 * (1.0 + lax.erf(inner * 0.7071067811865476))
            active = inner * below
            slope = below + inner * (jnp.exp(-0.5 * inner * inner) * 0.3989422804014327)
            p_ref[here, :] = (active * gate).astype(bf16)
            inner_grad = (product_grad * gate * slope).astype(bf16)
            gate_grad = (product_grad * active).astype(bf16)
            i_ref[here, :] = inner_grad
            t_ref[here, :] = gate_grad
            back = dot_rt(inner_grad, w_ref[:, :SPAN]) + dot_rt(gate_grad, w_ref[:, SPAN : 2 * SPAN])
            if place < 4:
                keep_ref[here, :] = back
            else:
                give_ref[(place - 4) * rows : (place - 2) * rows, :] = back.astype(bf16)

    shapes = (
        ((count, SPAN), bf16),
        ((count, SPAN), bf16),
        ((count, SPAN), bf16),
        ((count // 2, D), f32),
        ((count // 2, D), bf16),
    )
    arrays = (scalars, normed, grads, weight)
    return kernel_call(kernel, "feed_forward", shapes, arrays, (), 20)


def divided(block, bit):
    return (block >> bit) & 1, (block & ((1 << bit) - 1)) | ((block >> (bit + 1)) << bit)


def feed_grads(scalars, normed, grads, inner_grad, gate_grad, product, blocks):
    size = D // (2 * blocks)

    def kernel(scalar_ref, n_ref, o_ref, i_ref, t_ref, p_ref, *outs):
        for number in range(2 * blocks):
            columns = slice(number * size, (number + 1) * size)
            side, at = divided(number // 2, 0)
            ref, here = outs[2 * (number % 2) + side], slice(at * size, (at + 1) * size)
            grad = o_ref[:, columns]
            normed = n_ref[:, columns]
            ref[here, :SPAN] = dot_lt(normed, i_ref[...]).astype(bf16)
            ref[here, SPAN : 2 * SPAN] = dot_lt(normed, t_ref[...]).astype(bf16)
            ref[here, 2 * SPAN :] = dot_lt(grad, p_ref[...]).astype(bf16)

    shapes = (((D // 4, BLOCK), bf16),) * 4
    arrays = (scalars, normed, grads, inner_grad, gate_grad, product)
    outs = kernel_call(kernel, "feed_grads", shapes, arrays, limit=18)
    return (outs[:2], outs[2:])


def attend_back(scalars, parts, proj, probs, query, key, value, cosine, sine):
    rows = parts[0].shape[0]
    count, extended = query.shape[0], key.shape[0]
    block = 2 * HALF

    def kernel(scalar_ref, *refs):
        part_refs, refs = refs[:TEAM], refs[TEAM:]
        proj_ref, probs_ref, q_ref, k_ref, v_ref, cos_ref, sin_ref = refs[:7]
        out_ref, edge_ref, first_ref, last_ref, grad_ref, dk_ref, dv_ref = refs[7:]
        for place in range(0, TEAM, 2):
            both = jnp.concatenate([part_refs[place][...], part_refs[place + 1][...]], axis=0)
            both = dot(both, proj_ref[...]).astype(bf16)
            grad_ref[block_rows(scalar_ref, place, rows), :] = both[:rows]
            grad_ref[block_rows(scalar_ref, place + 1, rows), :] = both[rows:]
        lane = lax.broadcasted_iota(jnp.int32, (block, LANES), 1)
        dk_ref[...] = jnp.zeros_like(dk_ref)
        dv_ref[...] = jnp.zeros_like(dv_ref)
        for first in range(0, count, block):
            grad = grad_ref[first : first + block, :]
            query_low = q_ref[first : first + block, :]
            key_low = k_ref[first : first + 2 * block, :]
            value_low = v_ref[first : first + 2 * block, :]
            results = []
            key_sum = jnp.zeros((2 * block, LANES), f32)
            value_sum = jnp.zeros((2 * block, LANES), f32)
            for head in range(2):
                own_grad = only_head(grad, head)
                probs_low = probs_ref[head, first : first + block, :]
                probs = probs_low.astype(f32)
                probs_grad = dot_rt(own_grad, value_low)
                delta = jnp.sum(probs * probs_grad, axis=1, keepdims=True)
                scores_grad = (probs * (probs_grad - delta)).astype(bf16)
                results.append(dot(scores_grad, key_low))
                key_sum += dot_lt(scores_grad, only_head(query_low, head))
                value_sum += dot_lt(probs_low, own_grad)
            dk_ref[first : first + 2 * block, :] += key_sum * score_scale
            dv_ref[first : first + 2 * block, :] += value_sum
            query_grad = jnp.where(lane < HEAD_DIM, results[0], results[1]) * score_scale
            place = slice(first + HALF, first + HALF + block)
            out_ref[first : first + block, :LANES] = (
                query_grad * cos_ref[place, :] - turn(query_grad * sin_ref[place, :])
            ).astype(bf16)
        inner = slice(HALF, HALF + count)
        out_ref[:, LANES : 2 * LANES] = turned_back(dk_ref[inner, :], cos_ref, sin_ref, inner)
        out_ref[:, 2 * LANES :] = dv_ref[inner, :].astype(bf16)
        for i, place in enumerate((HALF, count)):
            edge_ref[i, :, :LANES] = dk_ref[place : place + HALF, :]
            edge_ref[i, :, LANES:] = dv_ref[place : place + HALF, :]
        for out, edge in ((first_ref, slice(0, HALF)), (last_ref, slice(extended - HALF, extended))):
            out[:, :LANES] = dk_ref[edge, :].astype(bf16)
            out[:, LANES:] = dv_ref[edge, :].astype(bf16)

    shapes = (
        ((count, 3 * LANES), bf16),
        ((2, HALF, 2 * LANES), f32),
        ((HALF, 2 * LANES), bf16),
        ((HALF, 2 * LANES), bf16),
    )
    arrays = (scalars, *parts, proj, probs, query, key, value, cosine, sine)
    scratch = (
        pltpu.VMEM((count, LANES), bf16),
        pltpu.VMEM((extended, LANES), f32),
        pltpu.VMEM((extended, LANES), f32),
    )
    return kernel_call(kernel, "attend_back", shapes, arrays, scratch, 18)


def turned_back(grad, cos_ref, sin_ref, place):
    return (grad * cos_ref[place, :] - turn(grad * sin_ref[place, :])).astype(bf16)


def join(scalars, grads, edge, before, behind, cosine, sine, rows):
    count = grads.shape[0]

    def kernel(scalar_ref, in_ref, edge_ref, before_ref, behind_ref, cos_ref, sin_ref, out_ref, team_ref):
        out_ref[...] = in_ref[...]
        for i, (ref, first) in enumerate(((before_ref, 0), (behind_ref, count - HALF))):
            total = edge_ref[i] + ref[...].astype(f32)
            here, place = slice(first, first + HALF), slice(first + HALF, first + 2 * HALF)
            out_ref[here, LANES : 2 * LANES] = turned_back(
                total[:, :LANES], cos_ref, sin_ref, place
            )
            out_ref[here, 2 * LANES :] = total[:, LANES:].astype(bf16)
        for place in range(TEAM):
            team_ref[place * rows : (place + 1) * rows, :] = out_ref[
                block_rows(scalar_ref, place, rows), :
            ]

    shapes = (((count, 3 * LANES), bf16),) * 2
    arrays = (scalars, grads, edge, before, behind, cosine, sine)
    return kernel_call(kernel, "join_halo", shapes, arrays, limit=10)


def head_grads(scalars, parts, normed, grads, attended, blocks):
    rows = parts[0].shape[0]
    size = D // blocks

    def kernel(scalar_ref, *refs):
        part_refs, refs = refs[:TEAM], refs[TEAM:]
        n_ref, g_ref, a_ref, keep_ref, give_ref, middle_ref, beside_ref = refs
        for place in range(TEAM):
            here = slice(place * rows, (place + 1) * rows)
            middle_ref[here, :] = part_refs[place][...]
            beside_ref[here, :] = a_ref[block_rows(scalar_ref, place, rows), :]
        for block in range(blocks):
            columns = slice(block * size, (block + 1) * size)
            side, at = divided(block, 0)
            ref, here = (keep_ref, give_ref)[side], slice(at * size, (at + 1) * size)
            ref[here, : 3 * LANES] = dot_lt(n_ref[:, columns], g_ref[...]).astype(bf16)
            ref[here, 3 * LANES :] = dot_lt(middle_ref[:, columns], beside_ref[...]).astype(bf16)

    count = TEAM * rows
    shapes = (((D // 2, 4 * LANES), bf16),) * 2
    scratch = (pltpu.VMEM((count, D), bf16), pltpu.VMEM((count, LANES), bf16))
    arrays = (scalars, *parts, normed, grads, attended)
    return kernel_call(kernel, "head_grads", shapes, arrays, scratch, 18)


def token_layout(first_token, count, total_tokens, document_starts):
    seq_length = total_tokens // document_starts.shape[0]
    global_ids = first_token + jnp.arange(count, dtype=jnp.int32)
    in_range = (global_ids >= 0) & (global_ids < total_tokens)
    safe_ids = jnp.clip(global_ids, 0, total_tokens - 1)
    sequence = safe_ids // seq_length
    place = safe_ids % seq_length
    starts = jnp.take(document_starts, sequence, axis=0)
    passed = starts <= place[:, None]
    segment = sequence * (document_starts.shape[1] + 1) + jnp.sum(passed.astype(jnp.int32), axis=1)
    segment = jnp.where(in_range, segment, -1)
    doc_place = place - jnp.max(jnp.where(passed, starts, 0), axis=1)
    return (segment, doc_place)


def rope_tables(doc_place):
    freq = rope_base ** (-(2.0 * jnp.arange(HEAD_DIM // 2, dtype=f32)) / HEAD_DIM)
    angles = doc_place.astype(f32)[:, None] * freq[None, :]
    spread = lambda table: jnp.tile(table, (1, LANES * 2 // HEAD_DIM))
    return (spread(jnp.cos(angles)), spread(jnp.sin(angles)))


def norm_parts(values):
    centre = values - jnp.mean(values, axis=-1, keepdims=True)
    spread = jnp.mean(centre * centre, axis=-1, keepdims=True)
    root = lax.rsqrt(spread + norm_eps)
    return (centre * root, root)


def norm_back(grad, gain, hat, root):
    scaled = grad * gain
    return root * (
        scaled
        - jnp.mean(scaled, axis=-1, keepdims=True)
        - hat * jnp.mean(scaled * hat, axis=-1, keepdims=True)
    )


def on_device(
    layer_input,
    qkv_weight,
    proj_weight,
    wide_weight,
    narrow_weight,
    first_gain,
    second_gain,
    output_grad,
    document_starts,
):
    size = lax.axis_size("dp")
    chips = size // 2
    bits = chips.bit_length() - 1
    far = tuple(range(2, bits))[::-1]
    device = lax.axis_index("dp").astype(jnp.int32)
    chip, core, member = device // 2, device % 2, device % TEAM
    near_key, far_key = chip % 4, chip - chip % 4
    is_first = core == 0
    rows = layer_input.shape[0]
    tokens = TEAM * rows
    own_rows = qkv_weight.shape[0]
    team_rows = TEAM * own_rows

    def to_team(parts):
        return [parts[0]] + [swap(parts[j], 2 * j) for j in (1, 2, 3)]

    def gather_team(value):
        near = to_team([value] * 4)
        return near + [swap(part, 1) for part in near]

    def both_sides(near):
        return near + [swap(part, 1) for part in near]

    def scatter_team(keeps, gives):
        got = swap(jnp.concatenate(gives, axis=0), 1)
        near = [
            jnp.concatenate(
                [
                    keep[j * rows : (j + 1) * rows]
                    + got[(4 * i + j) * rows : (4 * i + j + 1) * rows].astype(f32)
                    for i, keep in enumerate(keeps)
                ],
                axis=0,
            )
            for j in range(4)
        ]
        parts = [near[0]] + [part.astype(bf16) for part in near[1:]]
        got = to_team(parts)
        total = (got[0] + got[1].astype(f32)) + (got[2].astype(f32) + got[3].astype(f32))
        return total, got[1], parts[1]

    def deal_back(value):
        width = value.shape[1]
        value = value.astype(bf16).reshape(2, 2, 2 * own_rows, width)
        value = turned_by(value, near_key, (0, 1)).reshape(4, 2 * own_rows, width)
        parts = to_team([value[j] for j in range(4)])
        landed = parts[1]
        value = jnp.stack(parts, axis=0)
        value = turned_by(value.reshape(2, 2, 2, own_rows, width), core, (2,))
        value = jnp.stack([value[:, :, 0], swap(value[:, :, 1], 1)], axis=2)
        value = turned_by(value, member, (0, 1, 2)).astype(f32).reshape(TEAM, own_rows, width)
        return value, landed

    scalars = jnp.stack([member, far_key])
    zones = D // team_rows

    mine, give = pack(
        scalars, qkv_weight, proj_weight.T, wide_weight,
        jnp.pad(narrow_weight.T, ((0, 0), (0, -FF % LANES))),
        jnp.pad(
            jnp.stack([first_gain, second_gain]).astype(f32),
            ((0, 0), (UNITS, SPAN - UNITS - own_rows)),
        ),
    )
    both = jnp.stack([mine, swap(give, 1)], axis=1)
    parts = to_team([both[j] for j in range(4)])
    landed = parts[1]
    if own_rows % 16 == 0:
        head_rows, beside_rows, unit_rows = settle(scalars, parts)
    else:
        dealt = jnp.stack(parts, axis=0).reshape(2, 2, 2, own_rows, -1)
        dealt = turned_by(dealt, member, (0, 1, 2)).reshape(TEAM, own_rows, -1)
        at = 4 * LANES + UNITS
        gains = [dealt[:, i, at : at + own_rows].reshape(-1) for i in range(2)]
        gains = [jnp.pad(gain, (0, 2 * LANES - team_rows)).reshape(2, LANES) for gain in gains]
        dealt = dealt.reshape(team_rows, -1)
        head_rows, unit_rows = dealt[:, : 3 * LANES], dealt[:, 4 * LANES :]
        beside_rows = jnp.concatenate(
            [dealt[:, 3 * LANES : 4 * LANES], *gains, jnp.zeros((12, LANES), bf16)], axis=0
        )

    own_input = reorder(after(layer_input, parts), far_key, chips)
    inputs = gather_team(own_input)
    team_input = stack(scalars, inputs)
    team_first, team_last = edges(team_input, scalars, chips)
    before, behind = shifted(team_last, 1), shifted(team_first, -1)

    stages = []
    beside = gather_rows(beside_rows, far, 2, bits).reshape(zones, team_rows + 16, LANES)
    head_w = gather_rows(head_rows, far, 2, bits, None, stages)
    proj_w = beside[:, :team_rows].reshape(D, LANES)
    gain_one, gain_two = [
        beside[:, team_rows + i : team_rows + i + 2]
        .reshape(zones, -1)[:, :team_rows]
        .reshape(1, D)
        .astype(f32)
        for i in (0, 2)
    ]
    projs = to_team([proj_w] * 4)

    grad_late = after(output_grad, parts)
    out_grad = reorder(grad_late, far_key, chips)
    grads_low = to_team(
        [after(reorder(grad_late.astype(bf16), far_key, chips), inputs[3])] * 4
    )

    before, behind = reorder(before, far_key, chips), reorder(behind, far_key, chips)
    places = after(document_starts, both)
    segment, doc_place = token_layout(
        device // TEAM * tokens - HALF, tokens + 2 * HALF, rows * size, places
    )
    cosine, sine = rope_tables(doc_place)
    normed_low, query_low, key_low, value_low, probs, attended_low = attend(
        scalars, team_input, before, behind, gain_one, after(head_w, grads_low[1]), cosine, sine,
        segment[:, None], segment[None, :],
    )
    attended = gather_team(attended_low)
    projs = both_sides(after(projs, attended_low))
    out_low = stack(scalars, both_sides(after(grads_low, attended_low)))

    feed_w = gather_rows(after(unit_rows, stages[0]), far, 2, bits, (attended_low, head_w))
    normed_two, middle_own = mix(scalars, team_input, attended, projs, gain_two)
    inner_grad, gate_grad, product, keep, give = feed_forward(
        scalars, normed_two, out_low, feed_w
    )
    wide_back, landed, sent = scatter_team([keep], [give])
    feed_halves = feed_grads(
        scalars, after(normed_two, sent), out_low, inner_grad, gate_grad, product, zones
    )

    hat_own, root_own = norm_parts(middle_own)
    middle_grad = out_grad + norm_back(wide_back, gain_two, hat_own, root_own)
    middle = gather_team(after(middle_grad.astype(bf16), feed_halves))
    feed_got = [
        after(scatter_first(feed_halves[0], far), middle[1]),
        scatter_first(after(feed_halves[1], middle[1]), far),
    ]
    feed_half = [scatter_second(*pair) for pair in zip(feed_halves, feed_got)]
    own_grads, edge_grads, rim_first, rim_last = attend_back(
        after(scalars, feed_half[0]), middle, proj_w, probs, query_low, key_low, value_low, cosine, sine
    )
    from_before, from_behind = shifted(rim_last, 1), shifted(rim_first, -1)
    grads, team_grads = join(
        after(scalars, feed_half[1]), own_grads, edge_grads, from_before, from_behind, cosine, sine, rows
    )
    halves = head_grads(scalars, middle, normed_low, grads, attended_low, zones)
    late_product, team_grads = after((product, team_grads), halves)
    narrow_w = feed_w[:, 2 * SPAN :]
    half = tokens // 2
    back_sums, landed, sent = scatter_team(
        [dot_rt(team_grads[:half], head_w), dot_rt(late_product[:half], narrow_w)],
        [
            dot_rt(team_grads[half:], head_w).astype(bf16),
            dot_rt(late_product[half:], narrow_w).astype(bf16),
        ],
    )
    out_sum = back_sums[rows:]
    feed_first, feed_second = [
        scatter_rows(half, far, 2, bits, (back_sums,)) for half in feed_half
    ]
    feed_sums = jnp.concatenate([feed_first, feed_second], axis=0)
    first_back, late_sums = after((back_sums[:rows], feed_sums), feed_sums, landed)
    feed_shares, feed_landed = deal_back(late_sums)
    got = after(scatter_first(halves, far), landed)
    head_sums = scatter_rows(scatter_second(halves, got), far, 2, bits)
    hat_own, root_own = norm_parts(own_input.astype(f32))
    input_grad = reorder(
        middle_grad + norm_back(first_back, gain_one, hat_own, root_own), far_key, chips
    )
    layer_output = reorder((middle_own + out_sum).astype(bf16), far_key, chips)

    inner_share, gate_share, narrow_share = [
        feed_shares[:, :, i * SPAN : i * SPAN + UNITS].transpose(1, 0, 2).reshape(own_rows, FF)
        for i in range(3)
    ]
    wide_share = jnp.concatenate([inner_share, gate_share], axis=1)
    head_shares, landed = deal_back(after(head_sums, feed_landed))
    query_share, key_share, value_share, proj_share = [
        head_shares[:, :, i * LANES : (i + 1) * LANES].transpose(1, 0, 2).reshape(own_rows, D)
        for i in range(4)
    ]
    qkv_share = jnp.concatenate([query_share, key_share, value_share], axis=1)

    gain_one_share = jnp.sum(qkv_weight.astype(f32) * qkv_share, axis=1) / first_gain.astype(f32)
    gain_two_share = jnp.sum(wide_weight.astype(f32) * wide_share, axis=1) / second_gain.astype(f32)
    return (
        layer_output,
        input_grad,
        qkv_share,
        proj_share.T,
        wide_share,
        narrow_share.T,
        gain_one_share,
        gain_two_share,
    )


def solution(mesh):
    placed = (
        P("dp", None),
        P("dp", None),
        P(None, "dp"),
        P("dp", None),
        P(None, "dp"),
        P("dp"),
        P("dp"),
        P("dp", None),
        P(),
    )
    return jax.shard_map(
        on_device,
        mesh=mesh,
        in_specs=placed,
        out_specs=(
            P("dp", None),
            P("dp", None),
            P("dp", None),
            P(None, "dp"),
            P("dp", None),
            P(None, "dp"),
            P("dp"),
            P("dp"),
        ),
        check_vma=False,
    )
```
